32 devices in a mesh: group: 2 (over y), tx: 16 (over z, x, core).
Axes of the slice: x: 2, y: 2, z: 4, core: 2. Of those that a mesh axis runs over, the one named last changes fastest.
Arguments:
- pressure: float32 [32, 6, 8, 1024], P(('group', 'tx')), parts along dimension 0, may hold values from -4 to 4
- pressure_old: float32 [32, 6, 8, 1024], P(('group', 'tx')), parts along dimension 0, may hold values from -4 to 4
- soil_class: int32 [16, 6, 8, 1024], P('tx'), may hold values from 0 to 11
- elevation: float32 [16, 6, 1024], P('tx'), may hold values from -3 to 3
- land_mask: int32 [16, 6, 1024], P('tx'), may hold values 0 or 1
- rainfall: float32 [32, 6, 1024], P(('group', 'tx')), parts along dimension 0, may hold values from 0.1 to 1
- tile_list: int32 [16, 6], P('tx'), may hold values from -1 to 7, as said below
- neighbors: int32 [16, 6, 4], P('tx'), may hold values from -1 to 5, as said below
- atm_map: int32 [16, 6, 4], P('tx'), may hold values from -1 to 63, as said below
- forcing: float32 [2, 128, 256], P(None, ('group', 'tx')), parts along dimension 1, may hold values from 0.2 to 2
Outputs:
- pressure_new: float32 [32, 6, 8, 1024], P(('group', 'tx')), parts along dimension 0
- surface_return: float32 [32, 6, 4, 256], P(('group', 'tx')), parts along dimension 0
The draws below stay inside these ranges and needn't reach their ends.
There are 2 independent parts, one for each index of `group`. The reference program is written for one: setup_inputs(seed, part) draws one part's arguments, and reference() takes and returns one part's arrays. A program takes and returns all parts, laid end to end along the dimension named above; an argument that names none is the same for every part. Nothing has to cross between parts.
Inputs may be any that keep to these rules, and one draw needn't show every extreme that they name: `tile_list`: each tile row holds distinct tile columns in random slots; every tile row holds at least half of 6 tiles (and at least 2), and some tile row in every draw fills all 6 slots. `neighbors`: west and east name slots of the same tile row, north of tile row r-1, south of tile row r+1; -1 where the neighbouring tile column is empty, outside the domain, or the slot itself is empty. `atm_map`: atmosphere row a lives on index a // 4 of tx; the rows of one tile row that go to one index of tx all go to the same atmosphere row, and there are exactly 2 of them or none; -1 exactly for empty slots.
All inputs are finite; a program needn't handle non-finite values. No bound on the sum of `land_mask` on one device may be relied on, other than what follows from the above.
Results may differ from the reference program's by a relative error of at most 0.000067.
Values sent between devices are 32-bit elements; how exact they have to be, the bound alone decides.
A program may use at most 832 MiB of HBM per device.

```python
import math
import jax
import jax.numpy as jnp
import numpy as np
from jax import lax

TS = 32
NZ = 8
ITERS = 4
NCLASS = 12
TROWS = 16
TCOLS = 8
SLOTS = 6
ATM_DEV = 4
ATM_ROWS = 64
QROW = 256


def tile_layout(key):
    count_key, full_key, row_key, turn_key = jax.random.split(key, 4)
    fewest = max(2, SLOTS // 2)
    counts = jax.random.randint(count_key, (TROWS,), fewest, SLOTS + 1)
    full_row = jax.random.randint(full_key, (), 0, TROWS)
    counts = jnp.where(jnp.arange(TROWS) == full_row, SLOTS, counts)

    def one_row(subkey):
        first_key, second_key = jax.random.split(subkey)
        return (jax.random.permutation(first_key, TCOLS), jax.random.permutation(second_key, SLOTS))
    columns_drawn, slot_order = jax.vmap(one_row)(jax.random.split(row_key, TROWS))
    active = slot_order < counts[:, None]
    column = jnp.where(active, jnp.take_along_axis(columns_drawn, slot_order, axis=1), -1).astype(jnp.int32)
    matches = column[:, :, None] == jnp.arange(TCOLS)[None, None, :]
    holder = jnp.where(jnp.any(matches, axis=1), jnp.sum(matches * jnp.arange(SLOTS)[None, :, None], axis=1), -1)
    padded = jnp.pad(holder, ((1, 1), (1, 1)), constant_values=-1)
    row_index = jnp.arange(TROWS)[:, None] + 1
    col_place = jnp.maximum(column, 0) + 1
    west_slot = padded[row_index, col_place - 1]
    east_slot = padded[row_index, col_place + 1]
    north_slot = padded[row_index - 1, col_place]
    south_slot = padded[row_index + 1, col_place]
    link_table = jnp.stack([west_slot, east_slot, north_slot, south_slot], axis=-1)
    link_table = jnp.where(active[:, :, None], link_table, -1).astype(jnp.int32)
    rotation = jax.random.randint(turn_key, (TROWS // 4,), 0, TROWS)
    row_band = jnp.arange(TROWS) // 4
    pair_index = 2 * jnp.maximum(column, 0)[:, :, None] + jnp.arange(4)[None, None, :] // 2
    atm_device = (pair_index + rotation[row_band][:, None, None]) % TROWS
    target = atm_device * ATM_DEV + row_band[:, None, None]
    target = jnp.where(active[:, :, None], target, -1).astype(jnp.int32)
    return (column, link_table, target)


def draw_tile_list(key, part):
    layout = tile_layout(key)
    return layout[0]


def draw_neighbors(key, part):
    layout = tile_layout(key)
    return layout[1]


def draw_atm_map(key, part):
    layout = tile_layout(key)
    return layout[2]


def touch_ends(result, stream_key, low, high):
    shape = result.shape
    place = [jax.random.randint(jax.random.fold_in(stream_key, axis), (), 0, shape[axis]) for axis in range(len(shape))]
    result = result.at[tuple(place)].set(low)
    longest = shape.index(max(shape))
    place[longest] = (place[longest] + 1) % shape[longest]
    return result.at[tuple(place)].set(high)


def levels(own_key, dims, cuts, low, top_value):
    level, own = 1.0, jax.random.fold_in(own_key, 6)
    for axis_at, blocks in cuts:
        steps = jnp.exp(jax.random.uniform(jax.random.fold_in(own, axis_at), (blocks,), jnp.float32, low / len(cuts), top_value / len(cuts)))
        level = level * jnp.repeat(steps, dims[axis_at] // blocks).reshape([-1 if axis == axis_at else 1 for axis in range(len(dims))])
    return level


def bell_draw(key, shape, deviation, most, shards=(), held_as=jnp.bfloat16):
    factor_of = levels(key, shape, shards, -0.22, 0.18) if shards else 1.0
    values = jax.random.normal(key, shape, jnp.float32) * deviation * factor_of
    return jnp.minimum(jnp.maximum(values, -most), most).astype(held_as)


def setup_inputs(seed: int = 0, part: int = 0) -> dict:
    key_list = jax.random.split(jax.random.key(seed), 11)
    part_keys = jax.random.split(jax.random.fold_in(key_list[10], part), 11)
    pressure = bell_draw(part_keys[0], (TROWS, SLOTS, NZ, TS * TS), 1.0, 4.0, ((0, 16),), jnp.float32)
    pressure_old = bell_draw(part_keys[1], (TROWS, SLOTS, NZ, TS * TS), 1.0, 4.0, ((0, 16),), jnp.float32)
    soil_class = touch_ends(jax.random.randint(key_list[2], (TROWS, SLOTS, NZ, TS * TS), 0, NCLASS), jax.random.fold_in(key_list[2], 1), 0, NCLASS - 1).astype(jnp.int32)
    elevation = bell_draw(key_list[3], (TROWS, SLOTS, TS * TS), 0.5, 3.0, ((0, 16),), jnp.float32)
    land_mask = touch_ends((jax.random.randint(key_list[4], (TROWS, SLOTS, TS * TS), 0, 5) < 4).astype(jnp.int32), jax.random.fold_in(key_list[4], 1), 0, 1)
    rainfall = jnp.clip(jnp.exp(math.log(1.0) - 2.3025851 * jax.random.uniform(part_keys[5], (TROWS, SLOTS, TS * TS), jnp.float32) ** levels(part_keys[5], (TROWS, SLOTS, TS * TS), ((0, 16),), -0.2, 0.2)), 0.1, 1.0)
    tile_list = draw_tile_list(jax.random.fold_in(key_list[10], 71), part)
    neighbors = draw_neighbors(jax.random.fold_in(key_list[10], 71), part)
    atm_map = draw_atm_map(jax.random.fold_in(key_list[10], 71), part)
    forcing = jnp.clip(jnp.exp(math.log(2.0) - 2.3025851 * jax.random.uniform(part_keys[9], (2, ATM_ROWS, QROW), jnp.float32) ** levels(part_keys[9], (2, ATM_ROWS, QROW), ((1, 16),), -0.2, 0.2)), 0.2, 2.0)
    return {"pressure": pressure, "pressure_old": pressure_old, "soil_class": soil_class, "elevation": elevation, "land_mask": land_mask, "rainfall": rainfall, "tile_list": tile_list, "neighbors": neighbors, "atm_map": atm_map, "forcing": forcing}


KSAT = np.array([0.40, 0.32, 0.26, 0.21, 0.17, 0.14, 0.115, 0.095, 0.08, 0.067, 0.057, 0.05], np.float32)
SHAPE = np.array([3.0, 2.6, 2.2, 1.9, 1.6, 1.4, 1.2, 1.0, 0.9, 0.8, 0.7, 0.6], np.float32)
POROSITY = np.array([0.38, 0.39, 0.40, 0.43, 0.45, 0.41, 0.39, 0.43, 0.44, 0.38, 0.46, 0.48], np.float32)
SPECIFIC = 1.0
TIME_STEP = 4.0
LATERAL = 1.0
VERTICAL = 2.0
LAYER_DROP = 0.25
COUPLING = 0.5


def lookup(classes, values_table):
    summed = jnp.zeros(classes.shape, jnp.float32)
    for number in range(values_table.shape[0]):
        summed = summed + jnp.where(classes == number, float(values_table[number]), 0.0)
    return summed


def tile_edges(grid_field, tile_side):
    cell_count = grid_field.shape[-1]
    return (grid_field[..., tile_side - 1::tile_side], grid_field[..., 0::tile_side],
            grid_field[..., cell_count - tile_side:], grid_field[..., :tile_side])


def surrounding(grid_field, edge_set, tile_side):
    west_edge, east_edge, north_edge, south_edge = edge_set
    cell_count = grid_field.shape[-1]
    x_place = jnp.arange(cell_count) % tile_side
    y_place = jnp.arange(cell_count) // tile_side
    tile_reps = (1,) * (grid_field.ndim - 1) + (tile_side,)
    west_cells = jnp.where(x_place == 0, jnp.repeat(west_edge, tile_side, axis=-1), jnp.roll(grid_field, 1, axis=-1))
    east_cells = jnp.where(x_place == tile_side - 1, jnp.repeat(east_edge, tile_side, axis=-1), jnp.roll(grid_field, -1, axis=-1))
    north_cells = jnp.where(y_place == 0, jnp.tile(north_edge, tile_reps), jnp.roll(grid_field, tile_side, axis=-1))
    south_cells = jnp.where(y_place == tile_side - 1, jnp.tile(south_edge, tile_reps), jnp.roll(grid_field, -tile_side, axis=-1))
    upper_cells = jnp.concatenate([grid_field[..., :1, :], grid_field[..., :-1, :]], axis=-2)
    lower_cells = jnp.concatenate([grid_field[..., 1:, :], grid_field[..., -1:, :]], axis=-2)
    return [west_cells, east_cells, north_cells, south_cells, upper_cells, lower_cells]


def masks_for(present, layers, cell_count, tile_side):
    x_place = jnp.arange(cell_count) % tile_side
    y_place = jnp.arange(cell_count) // tile_side
    depth_index = jnp.arange(layers)[:, None]

    def edge_mask(at_edge, column):
        return jnp.where(at_edge, present[..., column][..., None, None], 1.0)

    return [edge_mask(x_place == 0, 0), edge_mask(x_place == tile_side - 1, 1),
            edge_mask(y_place == 0, 2), edge_mask(y_place == tile_side - 1, 3),
            jnp.where(depth_index > 0, 1.0, 0.0), jnp.where(depth_index < layers - 1, 1.0, 0.0)]


def row_balance(current, pressure_old, old_theta, saturated, shape_alpha, porosity, level, rainfall, present,
                near_head, near_sat, near_level, tile_side):
    layers, cell_count = current.shape[-2], current.shape[-1]
    face_masks = masks_for(present, layers, cell_count, tile_side)
    face_coefs = [LATERAL] * 4 + [VERTICAL] * 2
    relative = jax.nn.sigmoid(2.0 * current)
    conduct = saturated * relative
    slope_own = 2.0 * conduct * (1.0 - relative)
    potential = current + level
    inflow = jnp.zeros_like(current)
    conductance = jnp.zeros_like(current)
    face_store = []
    for head_j, sat_j, level_j, face_mask, face_coef in zip(near_head, near_sat, near_level, face_masks, face_coefs):
        relative_j = jax.nn.sigmoid(2.0 * head_j)
        weight = 0.5 * face_coef * face_mask
        face_k = weight * (conduct + sat_j * relative_j)
        head_drop = head_j + level_j - potential
        inflow = inflow + face_k * head_drop
        conductance = conductance + face_k
        face_store.append((face_k, weight * head_drop, 2.0 * sat_j * relative_j * (1.0 - relative_j)))
    theta_now = jax.nn.sigmoid(shape_alpha * current)
    storage = (SPECIFIC + porosity * shape_alpha * theta_now * (1.0 - theta_now)) / TIME_STEP
    depth_index = jnp.arange(layers)[:, None]
    surface = jnp.where(depth_index == 0, 1.0, 0.0) * rainfall[..., None, :]
    residual = (SPECIFIC * (current - pressure_old) + (porosity * theta_now - old_theta)) / TIME_STEP - inflow - surface
    return residual, storage + conductance, storage, slope_own, face_store


def apply_jacobian(step_field, near_step, slope_own, face_store, storage):
    jac_image = storage * step_field
    for (face_k, weighted_drop, slope_j), step_j in zip(face_store, near_step):
        jac_image = jac_image - face_k * (step_j - step_field) - weighted_drop * (slope_own * step_field + slope_j * step_j)
    return jac_image


def pick_slots(pool, chosen):
    return jax.vmap(lambda pool_rows, picks: pool_rows[jnp.maximum(picks, 0)])(pool, chosen)


def global_edges(grid_field, neighbors, tile_side):
    col_last, col_first, row_last, row_first = tile_edges(grid_field, tile_side)
    zero_rows = jnp.zeros_like(row_last[:1])
    from_north = jnp.concatenate([zero_rows, row_last[:-1]], axis=0)
    from_south = jnp.concatenate([row_first[1:], zero_rows], axis=0)
    return (pick_slots(col_last, neighbors[..., 0]), pick_slots(col_first, neighbors[..., 1]),
            pick_slots(from_north, neighbors[..., 2]), pick_slots(from_south, neighbors[..., 3]))


def reference(pressure, pressure_old, soil_class, elevation, land_mask, rainfall, tile_list, neighbors, atm_map, forcing):
    tile_side = TS
    row_count, slot_count, layers, cell_count = pressure.shape
    saturated = lookup(soil_class, KSAT)
    shape_alpha = lookup(soil_class, SHAPE)
    porosity = lookup(soil_class, POROSITY)
    depth_index = jnp.arange(layers)[:, None]
    level = elevation[:, :, None, :] - LAYER_DROP * depth_index.astype(jnp.float32)
    wet_cells = jnp.where((tile_list[:, :, None, None] >= 0) & (land_mask[:, :, None, :] > 0), 1.0, 0.0)
    present = jnp.where(neighbors >= 0, 1.0, 0.0)
    old_theta = porosity * jax.nn.sigmoid(shape_alpha * pressure_old)
    fixed_parts = (pressure_old, old_theta, saturated, shape_alpha, porosity, level, rainfall, present,
                   global_edges(saturated, neighbors, tile_side), global_edges(level, neighbors, tile_side))

    def balance_row(current, head_edges, parts):
        (one_old, one_theta, one_sat, one_alpha, one_poro, one_level, one_rain, one_present, sat_edges, level_edges) = parts
        return row_balance(current, one_old, one_theta, one_sat, one_alpha, one_poro, one_level, one_rain, one_present,
                           surrounding(current, head_edges, tile_side), surrounding(one_sat, sat_edges, tile_side),
                           surrounding(one_level, level_edges, tile_side), tile_side)

    def section_one(inputs):
        current, head_edges, parts = inputs
        residual, diagonal, storage, slope_own, face_store = balance_row(current, head_edges, parts)
        return residual, diagonal

    def section_two(inputs):
        current, head_edges, parts, step_field, step_edges, one_wet = inputs
        residual, diagonal, storage, slope_own, face_store = balance_row(current, head_edges, parts)
        jac_image = apply_jacobian(step_field, surrounding(step_field, step_edges, tile_side), slope_own, face_store, storage)
        return current - (step_field + one_wet * (residual - jac_image) / diagonal)

    for number in range(ITERS):
        head_edges = global_edges(pressure, neighbors, tile_side)
        residual, diagonal = lax.map(section_one, (pressure, head_edges, fixed_parts))
        step_field = wet_cells * residual / diagonal
        step_edges = global_edges(step_field, neighbors, tile_side)
        pressure = lax.map(section_two, (pressure, head_edges, fixed_parts, step_field, step_edges, wet_cells))

    relative_top = jax.nn.sigmoid(2.0 * pressure[:, :, 0, :])
    flux_rows = (wet_cells[:, :, 0, :] * saturated[:, :, 0, :] * relative_top).reshape(row_count * slot_count * 4, cell_count // 4)
    target = atm_map.reshape(-1)
    segment = jnp.where(target >= 0, target, ATM_ROWS)
    row_sums = jax.ops.segment_sum(flux_rows, segment, num_segments=ATM_ROWS + 1)[:ATM_ROWS]
    row_count_atm = jax.ops.segment_sum(jnp.ones(target.shape, jnp.float32), segment, num_segments=ATM_ROWS + 1)[:ATM_ROWS]
    row_mean = row_sums / jnp.maximum(row_count_atm, 1.0)[:, None]
    demand = forcing[0]
    supply = forcing[1]
    rate_rows = supply - demand * row_mean / (row_mean + demand)
    returned = jnp.where((target >= 0)[:, None], rate_rows[jnp.maximum(target, 0)], 0.0)
    surface_return = returned.reshape(row_count, slot_count, 4, cell_count // 4)
    top_layer = jnp.where(depth_index == 0, 1.0, 0.0)
    pressure_new = pressure + COUPLING * wet_cells * top_layer * returned.reshape(row_count, slot_count, 1, cell_count)
    return pressure_new, surface_return
```

```python
import functools

import jax
import jax.numpy as jnp
import numpy as np
from jax import lax
from jax.experimental import pallas as pl
from jax.experimental.pallas import tpu as pltpu
from jax.sharding import PartitionSpec as P

TS = 32
ITERS = 4
LANES = 128
HALO = 2 * ITERS * TS
STRIDE = 16

KSAT = np.array(
    [0.4, 0.32, 0.26, 0.21, 0.17, 0.14, 0.115, 0.095, 0.08, 0.067, 0.057, 0.05], np.float32
)
SHAPE = np.array([3.0, 2.6, 2.2, 1.9, 1.6, 1.4, 1.2, 1.0, 0.9, 0.8, 0.7, 0.6], np.float32)
POROSITY = np.array(
    [0.38, 0.39, 0.4, 0.43, 0.45, 0.41, 0.39, 0.43, 0.44, 0.38, 0.46, 0.48], np.float32
)
LAYER_DROP = 0.25
COUPLING = 0.5
MESH = pl.DeviceIdType.MESH


def sigmoid(v):
    return 1.0 / (1.0 + jnp.exp(-v))


def kernel(
    n,
    p_in,
    old_in,
    soil_in,
    elev_in,
    land_in,
    rain_in,
    tab_in,
    own_tab,
    forcing,
    p_out,
    ret_out,
    h,
    cst,
    soil,
    elev,
    land,
    rain,
    elev_rows,
    land_rows,
    rain_rows,
    north_vec,
    south_vec,
    north_tab,
    south_tab,
    kk,
    kp,
    hh,
    step,
    qq,
    wi,
    sat,
    alpha,
    poro,
    wet,
    kf_w,
    kf_e,
    kf_n,
    kf_s,
    kf_u,
    g_w,
    g_e,
    g_n,
    g_s,
    g_u,
    flux,
    rows,
    snd,
    rcv,
    snd2,
    rcv2,
    local_sem,
    send_sem,
    recv_sem,
    tab_sem,
    a_send,
    a_recv,
    b_send,
    b_recv,
    out_sem,
):
    me = lax.axis_index("tx")
    group = lax.axis_index("group")
    slots, layers = h.shape[0], h.shape[1]
    cells = p_in.shape[-1]
    own = pl.ds(HALO, cells)
    top_part, low_part = pl.ds(0, HALO), pl.ds(HALO + cells, HALO)
    atm = forcing.shape[1]
    hc = HALO // LANES
    nq = (cells + 2 * HALO) // LANES

    big = [(p_in, h), (old_in, cst), (soil_in, soil)]
    small = [(elev_in, elev), (land_in, land), (rain_in, rain)]
    local = []
    for src, dst in big:
        local.append((src.at[0], dst.at[:, :, own]))
    for src, dst in small:
        local.append((src.at[0], dst.at[:, own]))
    locals_ = [
        pltpu.make_async_copy(src, dst, local_sem.at[i]) for i, (src, dst) in enumerate(local)
    ]
    for copy in locals_:
        copy.start()

    for part in (top_part, low_part):
        for _, dst in big:
            dst[:, :, part] = jnp.zeros((slots, layers, HALO), dst.dtype)
        for _, dst in small:
            dst[:, part] = jnp.zeros((slots, HALO), dst.dtype)
    north_vec[...] = jnp.zeros(north_vec.shape, jnp.int32)
    south_vec[...] = jnp.zeros(south_vec.shape, jnp.int32)

    barrier = pltpu.get_barrier_semaphore()

    def greet(o, carry):
        pl.semaphore_signal(
            barrier, inc=1, device_id=(group, lax.rem(me + o, n)), device_id_type=MESH
        )
        return carry

    lax.fori_loop(1, n, greet, 0)
    pl.semaphore_wait(barrier, n - 1)

    def halo_copies(way):
        src_part = pl.ds(cells - HALO, HALO) if way == 0 else pl.ds(0, HALO)
        dst_part = top_part if way == 0 else low_part
        pairs = [(tab_in, north_vec if way == 0 else south_vec)]
        pairs += [(src.at[0, :, src_part], dst.at[:, dst_part]) for src, dst in small]
        pairs += [(src.at[0, :, :, src_part], dst.at[:, :, dst_part]) for src, dst in big]
        target = me + 1 if way == 0 else me - 1
        return [
            pltpu.make_async_remote_copy(
                src_ref=src,
                dst_ref=dst,
                send_sem=send_sem.at[way, i],
                recv_sem=recv_sem.at[way, i],
                device_id=(group, target),
                device_id_type=MESH,
            )
            for i, (src, dst) in enumerate(pairs)
        ]

    @pl.when(me < n - 1)
    def _():
        for copy in halo_copies(0):
            copy.start()

    @pl.when(me > 0)
    def _():
        for copy in halo_copies(1):
            copy.start()

    for copy in locals_:
        copy.wait()

    @pl.when(me > 0)
    def _():
        for copy in halo_copies(0):
            copy.wait_recv()

    @pl.when(me < n - 1)
    def _():
        for copy in halo_copies(1):
            copy.wait_recv()

    tabs = [
        pltpu.make_async_copy(north_vec, north_tab, tab_sem.at[0]),
        pltpu.make_async_copy(south_vec, south_tab, tab_sem.at[1]),
    ]
    for copy in tabs:
        copy.start()
    for copy in tabs:
        copy.wait()

    lane = lax.broadcasted_iota(jnp.int32, (layers, LANES), 1)
    layer = lax.broadcasted_iota(jnp.int32, (layers, LANES), 0)
    x_place = lax.rem(lane, TS)
    at_west, at_east = x_place == 0, x_place == TS - 1
    at_north, at_south = lane < TS, lane >= LANES - TS
    depth = layer.astype(jnp.float32) * LAYER_DROP
    upper = jnp.where(layer > 0, 2.0, 0.0)

    def table_of(q):
        return north_tab if q < hc else (own_tab if q < nq - hc else south_tab)

    def at(q):
        return pl.ds(q * LANES, LANES)

    def entry(q, s, f):
        return table_of(q)[0, s * STRIDE + f]

    def picks(s, first, last):
        found = {}
        for sec, q in ((0, 0), (1, hc), (2, nq - hc)):
            side = []
            for f in range(4):
                number = entry(q, s, f)
                side.append((jnp.maximum(number, 0), jnp.where(number >= 0, 1.0, 0.0)))
            found[sec] = side
        return found

    def section(q):
        return 0 if q < hc else (1 if q < nq - hc else 2)

    def around(field, s, q, found):
        side = found[section(q)]
        mid = field[s, :, at(q)]
        west = jnp.where(
            at_west,
            pltpu.roll(field[side[0][0], :, at(q)], LANES - TS + 1, 1),
            pltpu.roll(mid, 1, 1),
        )
        east = jnp.where(
            at_east,
            pltpu.roll(field[side[1][0], :, at(q)], TS - 1, 1),
            pltpu.roll(mid, LANES - 1, 1),
        )
        north_slot = side[2][0] if q in (hc, nq - hc) else s
        south_slot = side[3][0] if q in (hc - 1, nq - hc - 1) else s
        above = field[north_slot, :, at(max(q - 1, 0))]
        below = field[south_slot, :, at(min(q + 1, nq - 1))]
        north = pltpu.roll(jnp.where(at_south, above, mid), TS, 1)
        south = pltpu.roll(jnp.where(at_north, below, mid), LANES - TS, 1)
        return mid, west, east, north, south

    def conductivity(s, q, head):
        relative = sigmoid(2.0 * head)
        conduct = sat[s, :, at(q)] * relative
        kk[s, :, at(q)] = conduct
        kp[s, :, at(q)] = 2.0 * conduct * (1.0 - relative)

    def prepare(s, carry):
        for q in range(nq):
            classes = soil[s, :, at(q)]
            tables = [jnp.full((layers, LANES), float(t[0]), jnp.float32) for t in (KSAT, SHAPE, POROSITY)]
            for number in range(1, KSAT.shape[0]):
                hit = classes == number
                tables = [
                    jnp.where(hit, float(t[number]), v)
                    for t, v in zip((KSAT, SHAPE, POROSITY), tables)
                ]
            sat[s, :, at(q)] = 0.5 * tables[0]
            alpha[s, :, at(q)] = tables[1]
            poro[s, :, at(q)] = tables[2]
            old = cst[s, :, at(q)]
            rain_top = jnp.where(layer == 0, rain_rows[s, :, at(q)], 0.0)
            cst[s, :, at(q)] = 0.25 * (old + tables[2] * sigmoid(tables[1] * old)) + rain_top
            held = jnp.where(entry(q, s, 4) >= 0, 1.0, 0.0)
            wet[s, :, at(q)] = jnp.broadcast_to(
                jnp.where(land_rows[s, :, at(q)] > 0, held, 0.0), (layers, LANES)
            )
            head = h[s, :, at(q)]
            hh[s, :, at(q)] = head + (elev_rows[s, :, at(q)] - depth)
            conductivity(s, q, head)
        return carry

    for s in range(slots):
        for source, spread_rows in ((elev, elev_rows), (land, land_rows), (rain, rain_rows)):
            spread_rows[s] = source[s : s + 1, :]
    lax.fori_loop(0, slots, prepare, 0)

    def balance(first, last, s, carry):
        found = picks(s, first, last)
        for q in range(first, last):
            side = found[section(q)]
            k0, k_w, k_e, k_n, k_s = around(kk, s, q, found)
            h0, h_w, h_e, h_n, h_s = around(hh, s, q, found)
            mask_w = jnp.where(at_west, side[0][1], 1.0)
            mask_e = jnp.where(at_east, side[1][1], 1.0)
            mask_n = mask_s = None
            if q in (hc, nq - hc):
                mask_n = jnp.where(at_north, side[2][1], 1.0)
            if q == 0:
                mask_n = jnp.where(at_north, 0.0, 1.0)
            if q in (hc - 1, nq - hc - 1):
                mask_s = jnp.where(at_south, side[3][1], 1.0)
            if q == nq - 1:
                mask_s = jnp.where(at_south, 0.0, 1.0)
            inflow = None
            for k_j, h_j, mask, k_ref, g_ref in (
                (k_w, h_w, mask_w, kf_w, g_w),
                (k_e, h_e, mask_e, kf_e, g_e),
                (k_n, h_n, mask_n, kf_n, g_n),
                (k_s, h_s, mask_s, kf_s, g_s),
            ):
                face, drop = k0 + k_j, h_j - h0
                weighted = drop
                if mask is not None:
                    face, weighted = face * mask, drop * mask
                k_ref[s, :, at(q)] = face
                g_ref[s, :, at(q)] = weighted
                flow = face * drop
                inflow = flow if inflow is None else inflow + flow
                total = face if k_ref is kf_w else total + face
            drop = pltpu.roll(h0, 1, 0) - h0
            face = (k0 + pltpu.roll(k0, 1, 0)) * upper
            kf_u[s, :, at(q)] = face
            g_u[s, :, at(q)] = drop * upper
            flow = face * drop
            inflow = inflow + flow - pltpu.roll(flow, layers - 1, 0)
            total = total + face + pltpu.roll(face, layers - 1, 0)
            head = h[s, :, at(q)]
            shape = alpha[s, :, at(q)]
            pore = poro[s, :, at(q)]
            theta = sigmoid(shape * head)
            storage = 0.25 * (1.0 + pore * shape * theta * (1.0 - theta))
            residual = 0.25 * (head + pore * theta) - cst[s, :, at(q)] - inflow
            scaled = wet[s, :, at(q)] / (storage + total)
            move = scaled * residual
            wi[s, :, at(q)] = scaled
            step[s, :, at(q)] = move
            qq[s, :, at(q)] = kp[s, :, at(q)] * move
        return carry

    def advance(first, last, final, s, carry):
        found = picks(s, first, last)
        for q in range(first, last):
            s0, s_w, s_e, s_n, s_s = around(step, s, q, found)
            q0, q_w, q_e, q_n, q_s = around(qq, s, q, found)
            gsum = acc = None
            for s_j, q_j, k_ref, g_ref in (
                (s_w, q_w, kf_w, g_w),
                (s_e, q_e, kf_e, g_e),
                (s_n, q_n, kf_n, g_n),
                (s_s, q_s, kf_s, g_s),
            ):
                grad = g_ref[s, :, at(q)]
                term = k_ref[s, :, at(q)] * s_j + grad * q_j
                acc = term if acc is None else acc + term
                gsum = grad if gsum is None else gsum + grad
            face, grad = kf_u[s, :, at(q)], g_u[s, :, at(q)]
            acc = acc + face * pltpu.roll(s0, 1, 0) + grad * pltpu.roll(q0, 1, 0)
            acc = acc + pltpu.roll(face * s0 - grad * q0, layers - 1, 0)
            gsum = gsum + grad - pltpu.roll(grad, layers - 1, 0)
            change = s0 + wi[s, :, at(q)] * (acc + q0 * gsum)
            head = h[s, :, at(q)] - change
            h[s, :, at(q)] = head
            if final:
                strength = 2.0 * wet[s, :, at(q)] * sat[s, :, at(q)] * sigmoid(2.0 * head)
                half, part = divmod(q - hc, HALO // LANES)
                flux[s * 4 + half, :, pl.ds(part * LANES, LANES)] = strength[0:1]
            else:
                hh[s, :, at(q)] = hh[s, :, at(q)] - change
                conductivity(s, q, head)
        return carry

    rows_per = LANES // TS
    for number in range(ITERS):
        rows_a = 2 * ITERS - 1 - 2 * number
        rows_b = rows_a - 1
        wide_a, wide_b = -(-rows_a // rows_per), -(-rows_b // rows_per)
        lax.fori_loop(
            0, slots, functools.partial(balance, hc - wide_a, nq - hc + wide_a), 0
        )
        lax.fori_loop(
            0,
            slots,
            functools.partial(advance, hc - wide_b, nq - hc + wide_b, number == ITERS - 1),
            0,
        )

    quarter = flux.shape[-1]
    place = lax.broadcasted_iota(jnp.int32, (n, LANES), 0) * atm
    wide_place = lax.broadcasted_iota(jnp.int32, (n, quarter), 0) * atm

    def collect(s, carry):
        sums, label = carry
        for k in range(4):
            number = own_tab[0, s * STRIDE + 5 + k]
            there = number - wide_place
            hit = (there >= 0) & (there < atm)
            sums = sums + jnp.where(hit, flux[s * 4 + k], 0.0)
            there = number - place
            hit = (there >= 0) & (there < atm)
            label = jnp.where(hit, (there + 1).astype(jnp.float32), label)
        return sums, label

    sums, label = lax.fori_loop(
        0,
        slots,
        collect,
        (jnp.zeros((n, quarter), jnp.float32), jnp.zeros((n, LANES), jnp.float32)),
    )
    for d in range(n):
        snd[d, :, pl.ds(0, quarter)] = sums[d : d + 1]
        snd[d, :, pl.ds(quarter, LANES)] = label[d : d + 1]

    def exchange(src, dst, s_sem, r_sem):
        def one(o):
            peer = lax.rem(me + o, n)
            return pltpu.make_async_remote_copy(
                src_ref=src.at[peer],
                dst_ref=dst.at[me],
                send_sem=s_sem.at[o],
                recv_sem=r_sem.at[o],
                device_id=(group, peer),
                device_id_type=MESH,
            )

        def begin(o, carry):
            one(o).start()
            return carry

        def take(o, carry):
            source = lax.rem(me - o + n, n)
            pltpu.make_async_remote_copy(
                src_ref=src.at[source],
                dst_ref=dst.at[source],
                send_sem=s_sem.at[o],
                recv_sem=r_sem.at[o],
                device_id=(group, source),
                device_id_type=MESH,
            ).wait_recv()
            return carry

        def end(o, carry):
            one(o).wait_send()
            return carry

        lax.fori_loop(1, n, begin, 0)
        dst[me] = src[me]
        lax.fori_loop(1, n, take, 0)
        return lambda: lax.fori_loop(1, n, end, 0)

    finish_a = exchange(snd, rcv, a_send, a_recv)

    for d in range(n):
        rows[d : d + 1, :] = rcv[d]
    got = rows[:, pl.ds(0, quarter)]
    tag = rows[:, pl.ds(quarter, LANES)]
    tag = jnp.concatenate([tag] * (quarter // LANES), axis=1)

    back = jnp.zeros((n, quarter), jnp.float32)
    for a in range(atm):
        hit = tag == float(a + 1)
        total = jnp.sum(jnp.where(hit, got, 0.0), axis=0, keepdims=True)
        count = jnp.sum(jnp.where(hit, 2.0, 0.0), axis=0, keepdims=True)
        mean = total / jnp.maximum(count, 1.0)
        demand = forcing[0, a : a + 1, :]
        supply = forcing[1, a : a + 1, :]
        rate = supply - demand * mean / (mean + demand)
        back = jnp.where(hit, rate, back)

    for d in range(n):
        snd2[d] = back[d : d + 1]
    finish_b = exchange(snd2, rcv2, b_send, b_recv)

    def settle(s, carry):
        for k in range(4):
            number = own_tab[0, s * STRIDE + 5 + k]
            live = jnp.where(number >= 0, 1.0, 0.0)
            rate = rcv2[lax.div(jnp.maximum(number, 0), atm)] * live
            ret_out[0, s, pl.ds(k, 1), :] = rate
            for part in range(quarter // LANES):
                q = hc + k * (quarter // LANES) + part
                piece = rate[:, part * LANES : (part + 1) * LANES]
                h[s, :, at(q)] = h[s, :, at(q)] + jnp.where(
                    layer == 0, COUPLING * wet[s, :, at(q)] * piece, 0.0
                )
        return carry

    lax.fori_loop(0, slots, settle, 0)
    out = pltpu.make_async_copy(h.at[:, :, own], p_out.at[0], out_sem)
    out.start()
    finish_a()
    finish_b()

    @pl.when(me < n - 1)
    def _():
        for copy in halo_copies(0):
            copy.wait_send()

    @pl.when(me > 0)
    def _():
        for copy in halo_copies(1):
            copy.wait_send()

    out.wait()


def on_device(n, *args):
    (pressure, pressure_old, soil, elev, land, rain, tiles, neighbors, atm_map, forcing) = args
    _, slots, layers, cells = pressure.shape
    quarter = cells // 4
    wide = cells + 2 * HALO
    table = jnp.concatenate([neighbors[0], tiles[0][:, None], atm_map[0]], axis=1)
    table = jnp.pad(table, ((0, 0), (0, STRIDE - table.shape[1]))).reshape(1, slots * STRIDE)
    table = jnp.pad(table, ((0, 0), (0, -table.shape[1] % LANES)))
    width = table.shape[1]
    vec, smem, anywhere = pltpu.VMEM, pltpu.SMEM, pl.ANY

    def cube(kind=jnp.float32):
        return vec((slots, layers, wide), kind)

    def flat(kind=jnp.float32):
        return vec((slots, wide), kind)

    def lines(kind=jnp.float32):
        return vec((slots, 1, wide), kind)

    dma = pltpu.SemaphoreType.DMA
    return tuple(pl.pallas_call(
        functools.partial(kernel, n),
        out_shape=[
            jax.ShapeDtypeStruct(pressure.shape, jnp.float32),
            jax.ShapeDtypeStruct((1, slots, 4, quarter), jnp.float32),
        ],
        in_specs=[pl.BlockSpec(memory_space=anywhere)] * 7
        + [pl.BlockSpec(memory_space=smem), pl.BlockSpec(memory_space=vec)],
        out_specs=[pl.BlockSpec(memory_space=anywhere), pl.BlockSpec(memory_space=vec)],
        scratch_shapes=[
            cube(),
            cube(),
            cube(jnp.int32),
            flat(),
            flat(jnp.int32),
            flat(),
            lines(),
            lines(jnp.int32),
            lines(),
            vec((1, width), jnp.int32),
            vec((1, width), jnp.int32),
            smem((1, width), jnp.int32),
            smem((1, width), jnp.int32),
        ]
        + [cube()] * 20
        + [
            vec((slots * 4, 1, quarter), jnp.float32),
            vec((n, quarter + LANES), jnp.float32),
            vec((n, 1, quarter + LANES), jnp.float32),
            vec((n, 1, quarter + LANES), jnp.float32),
            vec((n, 1, quarter), jnp.float32),
            vec((n, 1, quarter), jnp.float32),
            dma((6,)),
            dma((2, 7)),
            dma((2, 7)),
            dma((2,)),
            dma((n,)),
            dma((n,)),
            dma((n,)),
            dma((n,)),
            dma,
        ],
        compiler_params=pltpu.CompilerParams(
            collective_id=0, has_side_effects=True, vmem_limit_bytes=60 * 2**20
        ),
    )(pressure, pressure_old, soil, elev, land, rain, table, table, forcing))


def solution(mesh):
    both = ("group", "tx")
    in_specs = (
        P(both, None, None, None),
        P(both, None, None, None),
        P("tx", None, None, None),
        P("tx", None, None),
        P("tx", None, None),
        P(both, None, None),
        P("tx", None),
        P("tx", None, None),
        P("tx", None, None),
        P(None, both, None),
    )
    out_specs = [P(both, None, None, None), P(both, None, None, None)]
    return jax.shard_map(
        functools.partial(on_device, mesh.shape["tx"]),
        mesh=mesh,
        in_specs=in_specs,
        out_specs=tuple(out_specs),
        check_vma=False,
    )
```

```python
import functools

import jax
import jax.numpy as jnp
import numpy as np
from jax import lax
from jax.experimental import pallas as pl
from jax.experimental.pallas import tpu as pltpu
from jax.sharding import PartitionSpec as P

TS = 32
ITERS = 4
LANES = 128
HALO = 2 * ITERS * TS

KSAT = np.array(
    [0.4, 0.32, 0.26, 0.21, 0.17, 0.14, 0.115, 0.095, 0.08, 0.067, 0.057, 0.05], np.float32
)
SHAPE = np.array([3.0, 2.6, 2.2, 1.9, 1.6, 1.4, 1.2, 1.0, 0.9, 0.8, 0.7, 0.6], np.float32)
POROSITY = np.array(
    [0.38, 0.39, 0.4, 0.43, 0.45, 0.41, 0.39, 0.43, 0.44, 0.38, 0.46, 0.48], np.float32
)
LAYER_DROP = 0.25
COUPLING = 0.5
MESH = pl.DeviceIdType.MESH


def sigmoid(v):
    return 1.0 / (1.0 + jnp.exp(-v))


def kernel(
    n,
    p_in,
    old_in,
    soil_in,
    elev_in,
    land_in,
    rain_in,
    nb_in,
    tile_in,
    atm_in,
    forcing_in,
    p_out,
    ret_out,
    h,
    cst,
    soil,
    elev,
    land,
    rain,
    north_nb_vec,
    south_nb_vec,
    north_tile_vec,
    south_tile_vec,
    north_nb,
    south_nb,
    north_tile,
    south_tile,
    own_nb,
    own_tile,
    own_atm,
    forcing,
    ret,
    kk,
    kp,
    hh,
    step,
    qq,
    wi,
    sat,
    alpha,
    poro,
    wet,
    kf_w,
    kf_e,
    kf_n,
    kf_s,
    kf_u,
    g_w,
    g_e,
    g_n,
    g_s,
    g_u,
    flux,
    rows,
    snd,
    rcv,
    snd2,
    rcv2,
    local_sem,
    send_sem,
    recv_sem,
    tab_sem,
    a_send,
    a_recv,
    b_send,
    b_recv,
    out_sem,
):
    me = lax.axis_index("tx")
    group = lax.axis_index("group")
    slots, layers = h.shape[0], h.shape[1]
    cells = p_in.shape[-1]
    own = pl.ds(HALO, cells)
    top_part, low_part = pl.ds(0, HALO), pl.ds(HALO + cells, HALO)
    atm = forcing.shape[1]
    hc = HALO // LANES
    nq = (cells + 2 * HALO) // LANES

    big = [(p_in, h), (old_in, cst), (soil_in, soil)]
    small = [(elev_in, elev), (land_in, land), (rain_in, rain)]
    local = []
    for src, dst in big:
        local.append((src.at[0], dst.at[:, :, own]))
    for src, dst in small:
        local.append((src, dst.at[:, :, own]))
    local += [(nb_in, own_nb), (tile_in, own_tile), (atm_in, own_atm), (forcing_in, forcing)]
    locals_ = [
        pltpu.make_async_copy(src, dst, local_sem.at[i]) for i, (src, dst) in enumerate(local)
    ]
    for copy in locals_:
        copy.start()

    for part in (top_part, low_part):
        for _, dst in big:
            dst[:, :, part] = jnp.zeros((slots, layers, HALO), dst.dtype)
        for _, dst in small:
            dst[:, :, part] = jnp.zeros((slots, 1, HALO), dst.dtype)
    for dst in (north_nb_vec, south_nb_vec, north_tile_vec, south_tile_vec):
        dst[...] = jnp.zeros(dst.shape, jnp.int32)

    barrier = pltpu.get_barrier_semaphore()

    def greet(o, carry):
        pl.semaphore_signal(
            barrier, inc=1, device_id=(group, lax.rem(me + o, n)), device_id_type=MESH
        )
        return carry

    lax.fori_loop(1, n, greet, 0)
    pl.semaphore_wait(barrier, n - 1)

    def halo_copies(way):
        src_part = pl.ds(cells - HALO, HALO) if way == 0 else pl.ds(0, HALO)
        dst_part = top_part if way == 0 else low_part
        pairs = [
            (nb_in, north_nb_vec if way == 0 else south_nb_vec),
            (tile_in, north_tile_vec if way == 0 else south_tile_vec),
        ]
        pairs += [(src.at[:, :, src_part], dst.at[:, :, dst_part]) for src, dst in small]
        pairs += [(src.at[0, :, :, src_part], dst.at[:, :, dst_part]) for src, dst in big]
        target = me + 1 if way == 0 else me - 1
        return [
            pltpu.make_async_remote_copy(
                src_ref=src,
                dst_ref=dst,
                send_sem=send_sem.at[way, i],
                recv_sem=recv_sem.at[way, i],
                device_id=(group, target),
                device_id_type=MESH,
            )
            for i, (src, dst) in enumerate(pairs)
        ]

    @pl.when(me < n - 1)
    def _():
        for copy in halo_copies(0):
            copy.start()

    @pl.when(me > 0)
    def _():
        for copy in halo_copies(1):
            copy.start()

    for copy in locals_:
        copy.wait()

    lane = lax.broadcasted_iota(jnp.int32, (layers, LANES), 1)
    layer = lax.broadcasted_iota(jnp.int32, (layers, LANES), 0)
    x_place = lax.rem(lane, TS)
    at_west, at_east = x_place == 0, x_place == TS - 1
    at_north, at_south = lane < TS, lane >= LANES - TS
    depth = layer.astype(jnp.float32) * LAYER_DROP
    upper = jnp.where(layer > 0, 2.0, 0.0)

    def at(q):
        return pl.ds(q * LANES, LANES)

    def neighbor(q, s, f):
        if hc <= q < nq - hc:
            return own_nb[0, f, s]
        return (north_nb if q < hc else south_nb)[0, f, s]

    def tile(q, s):
        return (north_tile if q < hc else (own_tile if q < nq - hc else south_tile))[0, s]

    def picks(s, first, last):
        found = {}
        for sec, q in ((0, 0), (1, hc), (2, nq - hc)):
            side = []
            for f in range(4):
                number = neighbor(q, s, f)
                side.append((jnp.maximum(number, 0), jnp.where(number >= 0, 1.0, 0.0)))
            found[sec] = side
        return found

    def section(q):
        return 0 if q < hc else (1 if q < nq - hc else 2)

    def around(field, s, q, found):
        side = found[section(q)]
        mid = field[s, :, at(q)]
        west = jnp.where(
            at_west,
            pltpu.roll(field[side[0][0], :, at(q)], LANES - TS + 1, 1),
            pltpu.roll(mid, 1, 1),
        )
        east = jnp.where(
            at_east,
            pltpu.roll(field[side[1][0], :, at(q)], TS - 1, 1),
            pltpu.roll(mid, LANES - 1, 1),
        )
        north_slot = side[2][0] if q in (hc, nq - hc) else s
        south_slot = side[3][0] if q in (hc - 1, nq - hc - 1) else s
        above = field[north_slot, :, at(max(q - 1, 0))]
        below = field[south_slot, :, at(min(q + 1, nq - 1))]
        north = pltpu.roll(jnp.where(at_south, above, mid), TS, 1)
        south = pltpu.roll(jnp.where(at_north, below, mid), LANES - TS, 1)
        return mid, west, east, north, south

    def conductivity(s, q, head):
        relative = sigmoid(2.0 * head)
        conduct = sat[s, :, at(q)] * relative
        kk[s, :, at(q)] = conduct
        kp[s, :, at(q)] = 2.0 * conduct * (1.0 - relative)

    def prepare(parts, s, carry):
        for q in parts:
            classes = soil[s, :, at(q)]
            tables = [jnp.full((layers, LANES), float(t[0]), jnp.float32) for t in (KSAT, SHAPE, POROSITY)]
            for number in range(1, KSAT.shape[0]):
                hit = classes == number
                tables = [
                    jnp.where(hit, float(t[number]), v)
                    for t, v in zip((KSAT, SHAPE, POROSITY), tables)
                ]
            sat[s, :, at(q)] = 0.5 * tables[0]
            alpha[s, :, at(q)] = tables[1]
            poro[s, :, at(q)] = tables[2]
            old = cst[s, :, at(q)]
            rain_top = jnp.where(layer == 0, rain[s, :, at(q)], 0.0)
            cst[s, :, at(q)] = 0.25 * (old + tables[2] * sigmoid(tables[1] * old)) + rain_top
            held = jnp.where(tile(q, s) >= 0, 1.0, 0.0)
            wet[s, :, at(q)] = jnp.broadcast_to(
                jnp.where(land[s, :, at(q)] > 0, held, 0.0), (layers, LANES)
            )
            head = h[s, :, at(q)]
            hh[s, :, at(q)] = head + (elev[s, :, at(q)] - depth)
            conductivity(s, q, head)
        return carry

    lax.fori_loop(0, slots, functools.partial(prepare, range(hc, nq - hc)), 0)

    @pl.when(me > 0)
    def _():
        for copy in halo_copies(0):
            copy.wait_recv()

    @pl.when(me < n - 1)
    def _():
        for copy in halo_copies(1):
            copy.wait_recv()

    tabs = [
        pltpu.make_async_copy(src, dst, tab_sem.at[i])
        for i, (src, dst) in enumerate(
            (
                (north_nb_vec, north_nb),
                (south_nb_vec, south_nb),
                (north_tile_vec, north_tile),
                (south_tile_vec, south_tile),
            )
        )
    ]
    for copy in tabs:
        copy.start()
    for copy in tabs:
        copy.wait()

    halo_parts = tuple(range(hc)) + tuple(range(nq - hc, nq))
    lax.fori_loop(0, slots, functools.partial(prepare, halo_parts), 0)

    def balance(first, last, s, carry):
        found = picks(s, first, last)
        for q in range(first, last):
            side = found[section(q)]
            k0, k_w, k_e, k_n, k_s = around(kk, s, q, found)
            h0, h_w, h_e, h_n, h_s = around(hh, s, q, found)
            mask_w = jnp.where(at_west, side[0][1], 1.0)
            mask_e = jnp.where(at_east, side[1][1], 1.0)
            mask_n = mask_s = None
            if q in (hc, nq - hc):
                mask_n = jnp.where(at_north, side[2][1], 1.0)
            if q == 0:
                mask_n = jnp.where(at_north, 0.0, 1.0)
            if q in (hc - 1, nq - hc - 1):
                mask_s = jnp.where(at_south, side[3][1], 1.0)
            if q == nq - 1:
                mask_s = jnp.where(at_south, 0.0, 1.0)
            inflow = None
            for k_j, h_j, mask, k_ref, g_ref in (
                (k_w, h_w, mask_w, kf_w, g_w),
                (k_e, h_e, mask_e, kf_e, g_e),
                (k_n, h_n, mask_n, kf_n, g_n),
                (k_s, h_s, mask_s, kf_s, g_s),
            ):
                face, drop = k0 + k_j, h_j - h0
                weighted = drop
                if mask is not None:
                    face, weighted = face * mask, drop * mask
                k_ref[s, :, at(q)] = face
                g_ref[s, :, at(q)] = weighted
                flow = face * drop
                inflow = flow if inflow is None else inflow + flow
                total = face if k_ref is kf_w else total + face
            drop = pltpu.roll(h0, 1, 0) - h0
            face = (k0 + pltpu.roll(k0, 1, 0)) * upper
            kf_u[s, :, at(q)] = face
            g_u[s, :, at(q)] = drop * upper
            flow = face * drop
            inflow = inflow + flow - pltpu.roll(flow, layers - 1, 0)
            total = total + face + pltpu.roll(face, layers - 1, 0)
            head = h[s, :, at(q)]
            shape = alpha[s, :, at(q)]
            pore = poro[s, :, at(q)]
            theta = sigmoid(shape * head)
            storage = 0.25 * (1.0 + pore * shape * theta * (1.0 - theta))
            residual = 0.25 * (head + pore * theta) - cst[s, :, at(q)] - inflow
            scaled = wet[s, :, at(q)] / (storage + total)
            move = scaled * residual
            wi[s, :, at(q)] = scaled
            step[s, :, at(q)] = move
            qq[s, :, at(q)] = kp[s, :, at(q)] * move
        return carry

    def advance(first, last, final, s, carry):
        found = picks(s, first, last)
        for q in range(first, last):
            s0, s_w, s_e, s_n, s_s = around(step, s, q, found)
            q0, q_w, q_e, q_n, q_s = around(qq, s, q, found)
            gsum = acc = None
            for s_j, q_j, k_ref, g_ref in (
                (s_w, q_w, kf_w, g_w),
                (s_e, q_e, kf_e, g_e),
                (s_n, q_n, kf_n, g_n),
                (s_s, q_s, kf_s, g_s),
            ):
                grad = g_ref[s, :, at(q)]
                term = k_ref[s, :, at(q)] * s_j + grad * q_j
                acc = term if acc is None else acc + term
                gsum = grad if gsum is None else gsum + grad
            face, grad = kf_u[s, :, at(q)], g_u[s, :, at(q)]
            acc = acc + face * pltpu.roll(s0, 1, 0) + grad * pltpu.roll(q0, 1, 0)
            acc = acc + pltpu.roll(face * s0 - grad * q0, layers - 1, 0)
            gsum = gsum + grad - pltpu.roll(grad, layers - 1, 0)
            change = s0 + wi[s, :, at(q)] * (acc + q0 * gsum)
            head = h[s, :, at(q)] - change
            h[s, :, at(q)] = head
            if final:
                strength = 2.0 * wet[s, :, at(q)] * sat[s, :, at(q)] * sigmoid(2.0 * head)
                half, part = divmod(q - hc, HALO // LANES)
                flux[s * 4 + half, :, pl.ds(part * LANES, LANES)] = strength[0:1]
            else:
                hh[s, :, at(q)] = hh[s, :, at(q)] - change
                conductivity(s, q, head)
        return carry

    rows_per = LANES // TS
    for number in range(ITERS):
        rows_a = 2 * ITERS - 1 - 2 * number
        rows_b = rows_a - 1
        wide_a, wide_b = -(-rows_a // rows_per), -(-rows_b // rows_per)
        lax.fori_loop(
            0, slots, functools.partial(balance, hc - wide_a, nq - hc + wide_a), 0
        )
        lax.fori_loop(
            0,
            slots,
            functools.partial(advance, hc - wide_b, nq - hc + wide_b, number == ITERS - 1),
            0,
        )

    quarter = flux.shape[-1]
    place = lax.broadcasted_iota(jnp.int32, (n, LANES), 0) * atm
    wide_place = lax.broadcasted_iota(jnp.int32, (n, quarter), 0) * atm

    def collect(s, carry):
        sums, label = carry
        for k in range(4):
            number = own_atm[0, k, s]
            there = number - wide_place
            hit = (there >= 0) & (there < atm)
            sums = sums + jnp.where(hit, flux[s * 4 + k], 0.0)
            there = number - place
            hit = (there >= 0) & (there < atm)
            label = jnp.where(hit, (there + 1).astype(jnp.float32), label)
        return sums, label

    sums, label = lax.fori_loop(
        0,
        slots,
        collect,
        (jnp.zeros((n, quarter), jnp.float32), jnp.zeros((n, LANES), jnp.float32)),
    )
    for d in range(n):
        snd[d, :, pl.ds(0, quarter)] = sums[d : d + 1]
        snd[d, :, pl.ds(quarter, LANES)] = label[d : d + 1]

    def exchange(src, dst, s_sem, r_sem):
        def one(o):
            peer = lax.rem(me + o, n)
            return pltpu.make_async_remote_copy(
                src_ref=src.at[peer],
                dst_ref=dst.at[me],
                send_sem=s_sem,
                recv_sem=r_sem,
                device_id=(group, peer),
                device_id_type=MESH,
            )

        def begin(o, carry):
            one(o).start()
            return carry

        lax.fori_loop(1, n, begin, 0)
        dst[me] = src[me]
        everyone = pltpu.make_async_copy(
            src.at[pl.ds(0, n - 1)], dst.at[pl.ds(0, n - 1)], r_sem
        )
        everyone.wait()
        return lambda: pltpu.make_async_copy(
            src.at[pl.ds(0, n - 1)], dst.at[pl.ds(0, n - 1)], s_sem
        ).wait()

    finish_a = exchange(snd, rcv, a_send, a_recv)

    for d in range(n):
        rows[d : d + 1, :] = rcv[d]
    got = rows[:, pl.ds(0, quarter)]
    tag = rows[:, pl.ds(quarter, LANES)]
    tag = jnp.concatenate([tag] * (quarter // LANES), axis=1)

    back = jnp.zeros((n, quarter), jnp.float32)
    for a in range(atm):
        hit = tag == float(a + 1)
        total = jnp.sum(jnp.where(hit, got, 0.0), axis=0, keepdims=True)
        count = jnp.sum(jnp.where(hit, 2.0, 0.0), axis=0, keepdims=True)
        mean = total / jnp.maximum(count, 1.0)
        demand = forcing[0, a : a + 1, :]
        supply = forcing[1, a : a + 1, :]
        rate = supply - demand * mean / (mean + demand)
        back = jnp.where(hit, rate, back)

    for d in range(n):
        snd2[d] = back[d : d + 1]
    finish_b = exchange(snd2, rcv2, b_send, b_recv)

    def settle(s, carry):
        for k in range(4):
            number = own_atm[0, k, s]
            live = jnp.where(number >= 0, 1.0, 0.0)
            rate = rcv2[lax.div(jnp.maximum(number, 0), atm)] * live
            ret[0, s, pl.ds(k, 1), :] = rate
            for part in range(quarter // LANES):
                q = hc + k * (quarter // LANES) + part
                piece = rate[:, part * LANES : (part + 1) * LANES]
                h[s, :, at(q)] = h[s, :, at(q)] + jnp.where(
                    layer == 0, COUPLING * wet[s, :, at(q)] * piece, 0.0
                )
        return carry

    lax.fori_loop(0, slots, settle, 0)
    outs = [
        pltpu.make_async_copy(h.at[:, :, own], p_out.at[0], out_sem.at[0]),
        pltpu.make_async_copy(ret, ret_out, out_sem.at[1]),
    ]
    for copy in outs:
        copy.start()
    finish_a()
    finish_b()

    @pl.when(me < n - 1)
    def _():
        for copy in halo_copies(0):
            copy.wait_send()

    @pl.when(me > 0)
    def _():
        for copy in halo_copies(1):
            copy.wait_send()

    for copy in outs:
        copy.wait()


def copy_kernel(*refs):
    count = len(refs) // 2
    sems = refs[-1]
    copies = [
        pltpu.make_async_copy(refs[i], refs[count + i], sems.at[i]) for i in range(count)
    ]
    for copy in copies:
        copy.start()
    for copy in copies:
        copy.wait()


def hand_over(arrays):
    return pl.pallas_call(
        copy_kernel,
        out_shape=[jax.ShapeDtypeStruct(v.shape, v.dtype) for v in arrays],
        in_specs=[pl.BlockSpec(memory_space=pl.ANY)] * len(arrays),
        out_specs=[pl.BlockSpec(memory_space=pl.ANY)] * len(arrays),
        scratch_shapes=[pltpu.SemaphoreType.DMA((len(arrays),))],
        compiler_params=pltpu.CompilerParams(vmem_limit_bytes=60 * 2**20),
    )(*arrays)


def on_device(n, *args):
    (pressure, pressure_old, soil, elev, land, rain, tiles, neighbors, atm_map, forcing) = args
    _, slots, layers, cells = pressure.shape
    quarter = cells // 4
    wide = cells + 2 * HALO
    elev, land, rain = (jnp.transpose(v, (1, 0, 2)) for v in (elev, land, rain))
    neighbors, atm_map = (jnp.transpose(v, (0, 2, 1)) for v in (neighbors, atm_map))
    vec, smem, anywhere = pltpu.VMEM, pltpu.SMEM, pl.ANY

    def cube(kind=jnp.float32):
        return vec((slots, layers, wide), kind)

    def lines(kind=jnp.float32):
        return vec((slots, 1, wide), kind)

    dma = pltpu.SemaphoreType.DMA
    made = pl.pallas_call(
        functools.partial(kernel, n),
        out_shape=[
            jax.ShapeDtypeStruct(pressure.shape, jnp.float32),
            jax.ShapeDtypeStruct((1, slots, 4, quarter), jnp.float32),
        ],
        in_specs=[pl.BlockSpec(memory_space=anywhere)] * 10,
        out_specs=[pl.BlockSpec(memory_space=anywhere)] * 2,
        scratch_shapes=[
            cube(),
            cube(),
            cube(jnp.int32),
            lines(),
            lines(jnp.int32),
            lines(),
            vec((1, 4, slots), jnp.int32),
            vec((1, 4, slots), jnp.int32),
            vec((1, slots), jnp.int32),
            vec((1, slots), jnp.int32),
            smem((1, 4, slots), jnp.int32),
            smem((1, 4, slots), jnp.int32),
            smem((1, slots), jnp.int32),
            smem((1, slots), jnp.int32),
            smem((1, 4, slots), jnp.int32),
            smem((1, slots), jnp.int32),
            smem((1, 4, slots), jnp.int32),
            vec(forcing.shape, jnp.float32),
            vec((1, slots, 4, quarter), jnp.float32),
        ]
        + [cube()] * 20
        + [
            vec((slots * 4, 1, quarter), jnp.float32),
            vec((n, quarter + LANES), jnp.float32),
            vec((n, 1, quarter + LANES), jnp.float32),
            vec((n, 1, quarter + LANES), jnp.float32),
            vec((n, 1, quarter), jnp.float32),
            vec((n, 1, quarter), jnp.float32),
            dma((10,)),
            dma((2, 8)),
            dma((2, 8)),
            dma((4,)),
            dma,
            dma,
            dma,
            dma,
            dma((2,)),
        ],
        compiler_params=pltpu.CompilerParams(
            collective_id=0, has_side_effects=True, vmem_limit_bytes=60 * 2**20
        ),
    )(pressure, pressure_old, soil, elev, land, rain, neighbors, tiles, atm_map, forcing)
    return tuple(hand_over(made))


def solution(mesh):
    both = ("group", "tx")
    in_specs = (
        P(both, None, None, None),
        P(both, None, None, None),
        P("tx", None, None, None),
        P("tx", None, None),
        P("tx", None, None),
        P(both, None, None),
        P("tx", None),
        P("tx", None, None),
        P("tx", None, None),
        P(None, both, None),
    )
    out_specs = [P(both, None, None, None), P(both, None, None, None)]
    return jax.shard_map(
        functools.partial(on_device, mesh.shape["tx"]),
        mesh=mesh,
        in_specs=in_specs,
        out_specs=tuple(out_specs),
        check_vma=False,
    )
```

```python
import functools

import jax
import jax.numpy as jnp
import numpy as np
from jax import lax
from jax.experimental import pallas as pl
from jax.experimental.pallas import tpu as pltpu
from jax.sharding import PartitionSpec as P

TS = 32
ITERS = 4
LANES = 128
HALO = 2 * ITERS * TS

KSAT = np.array(
    [0.4, 0.32, 0.26, 0.21, 0.17, 0.14, 0.115, 0.095, 0.08, 0.067, 0.057, 0.05], np.float32
)
SHAPE = np.array([3.0, 2.6, 2.2, 1.9, 1.6, 1.4, 1.2, 1.0, 0.9, 0.8, 0.7, 0.6], np.float32)
POROSITY = np.array(
    [0.38, 0.39, 0.4, 0.43, 0.45, 0.41, 0.39, 0.43, 0.44, 0.38, 0.46, 0.48], np.float32
)
LAYER_DROP = 0.25
COUPLING = 0.5
MESH = pl.DeviceIdType.MESH


def inverse(v):
    guess = pl.reciprocal(v, approx=True)
    return guess * (2.0 - v * guess)


def kernel(
    n,
    p_in,
    old_in,
    soil_in,
    elev_in,
    land_in,
    rain_in,
    nb_in,
    tile_in,
    atm_in,
    forcing_in,
    p_out,
    added_out,
    ret_out,
    h,
    cst,
    soil,
    elev,
    land,
    rain,
    north_nb_vec,
    south_nb_vec,
    north_tile_vec,
    south_tile_vec,
    north_nb,
    south_nb,
    north_tile,
    south_tile,
    own_nb,
    own_tile,
    own_atm,
    forcing,
    ret,
    added,
    kk,
    kp,
    hh,
    step,
    qq,
    wi,
    sat,
    alpha,
    poro,
    wet,
    kf_w,
    kf_e,
    kf_n,
    kf_s,
    kf_u,
    g_w,
    g_e,
    g_n,
    g_s,
    g_u,
    flux,
    rows,
    snd,
    rcv,
    snd2,
    rcv2,
    local_sem,
    send_sem,
    recv_sem,
    tab_sem,
    a_send,
    a_recv,
    b_send,
    b_recv,
    out_sem,
):
    me = lax.axis_index("tx")
    group = lax.axis_index("group")
    slots, layers = h.shape[0], h.shape[1]
    cells = p_in.shape[-1]
    own = pl.ds(HALO, cells)
    top_part, low_part = pl.ds(0, HALO), pl.ds(HALO + cells, HALO)
    atm = forcing.shape[1]
    hc = HALO // LANES
    nq = (cells + 2 * HALO) // LANES

    big = [(p_in, h), (old_in, cst), (soil_in, soil)]
    small = [(elev_in, elev), (land_in, land), (rain_in, rain)]
    local = []
    for src, dst in big:
        local.append((src.at[0], dst.at[:, :, own]))
    for src, dst in small:
        local.append((src, dst.at[:, :, own]))
    local += [(nb_in, own_nb), (tile_in, own_tile), (atm_in, own_atm), (forcing_in, forcing)]
    locals_ = [
        pltpu.make_async_copy(src, dst, local_sem.at[i]) for i, (src, dst) in enumerate(local)
    ]
    for copy in locals_:
        copy.start()

    for part in (top_part, low_part):
        for _, dst in big:
            dst[:, :, part] = jnp.zeros((slots, layers, HALO), dst.dtype)
        for _, dst in small:
            dst[:, :, part] = jnp.zeros((slots, 1, HALO), dst.dtype)
    for dst in (north_nb_vec, south_nb_vec, north_tile_vec, south_tile_vec):
        dst[...] = jnp.zeros(dst.shape, jnp.int32)

    barrier = pltpu.get_barrier_semaphore()

    def greet(o, carry):
        pl.semaphore_signal(
            barrier, inc=1, device_id=(group, lax.rem(me + o, n)), device_id_type=MESH
        )
        return carry

    lax.fori_loop(1, n, greet, 0, unroll=n <= 32)
    pl.semaphore_wait(barrier, n - 1)

    def halo_copies(way):
        src_part = pl.ds(cells - HALO, HALO) if way == 0 else pl.ds(0, HALO)
        dst_part = top_part if way == 0 else low_part
        pairs = [
            (nb_in, north_nb_vec if way == 0 else south_nb_vec),
            (tile_in, north_tile_vec if way == 0 else south_tile_vec),
        ]
        pairs += [(src.at[:, :, src_part], dst.at[:, :, dst_part]) for src, dst in small]
        pairs += [(src.at[0, :, :, src_part], dst.at[:, :, dst_part]) for src, dst in big]
        target = me + 1 if way == 0 else me - 1
        return [
            pltpu.make_async_remote_copy(
                src_ref=src,
                dst_ref=dst,
                send_sem=send_sem.at[way, i],
                recv_sem=recv_sem.at[way, i],
                device_id=(group, target),
                device_id_type=MESH,
            )
            for i, (src, dst) in enumerate(pairs)
        ]

    @pl.when(me < n - 1)
    def _():
        for copy in halo_copies(0):
            copy.start()

    @pl.when(me > 0)
    def _():
        for copy in halo_copies(1):
            copy.start()

    for copy in locals_:
        copy.wait()

    lane = lax.broadcasted_iota(jnp.int32, (layers, LANES), 1)
    layer = lax.broadcasted_iota(jnp.int32, (layers, LANES), 0)
    x_place = lax.rem(lane, TS)
    at_west, at_east = x_place == 0, x_place == TS - 1
    at_north, at_south = lane < TS, lane >= LANES - TS
    depth = layer.astype(jnp.float32) * LAYER_DROP
    upper = jnp.where(layer > 0, 2.0, 0.0)

    def at(q):
        return pl.ds(q * LANES, LANES)

    def neighbor(q, s, f):
        if hc <= q < nq - hc:
            return own_nb[0, f, s]
        return (north_nb if q < hc else south_nb)[0, f, s]

    def tile(q, s):
        return (north_tile if q < hc else (own_tile if q < nq - hc else south_tile))[0, s]

    def picks(s, parts):
        found = {}
        for sec, q in ((0, 0), (1, hc), (2, nq - hc)):
            if all(section(part) != sec for part in parts):
                continue
            side = []
            for f in range(4):
                number = neighbor(q, s, f)
                side.append((jnp.maximum(number, 0), jnp.where(number >= 0, 1.0, 0.0)))
            found[sec] = side
        return found

    def section(q):
        return 0 if q < hc else (1 if q < nq - hc else 2)

    def around(field, s, q, found):
        side = found[section(q)]
        mid = field[s, :, at(q)]
        west = jnp.where(
            at_west,
            pltpu.roll(field[side[0][0], :, at(q)], LANES - TS + 1, 1),
            pltpu.roll(mid, 1, 1),
        )
        east = jnp.where(
            at_east,
            pltpu.roll(field[side[1][0], :, at(q)], TS - 1, 1),
            pltpu.roll(mid, LANES - 1, 1),
        )
        north_slot = side[2][0] if q in (hc, nq - hc) else s
        south_slot = side[3][0] if q in (hc - 1, nq - hc - 1) else s
        above = field[north_slot, :, at(max(q - 1, 0))]
        below = field[south_slot, :, at(min(q + 1, nq - 1))]
        north = pltpu.roll(jnp.where(at_south, above, mid), TS, 1)
        south = pltpu.roll(jnp.where(at_north, below, mid), LANES - TS, 1)
        return mid, west, east, north, south

    def conductivity(s, q, head):
        bend = jnp.tanh(head)
        conduct = sat[s, :, at(q)] * (1.0 + bend)
        kk[s, :, at(q)] = conduct
        kp[s, :, at(q)] = conduct * (1.0 - bend)

    def prepare(parts, s, carry):
        for q in parts:
            classes = soil[s, :, at(q)]
            tables = [jnp.full((layers, LANES), float(t[0]), jnp.float32) for t in (KSAT, SHAPE, POROSITY)]
            for number in range(1, KSAT.shape[0]):
                hit = classes == number
                tables = [
                    jnp.where(hit, float(t[number]), v)
                    for t, v in zip((KSAT, SHAPE, POROSITY), tables)
                ]
            sat[s, :, at(q)] = 0.25 * tables[0]
            half_shape, eighth = 0.5 * tables[1], 0.125 * tables[2]
            alpha[s, :, at(q)] = half_shape
            poro[s, :, at(q)] = eighth
            old = cst[s, :, at(q)]
            rain_top = jnp.where(layer == 0, rain[s, :, at(q)], 0.0)
            cst[s, :, at(q)] = 0.25 * old + eighth * jnp.tanh(half_shape * old) + rain_top
            held = jnp.where(tile(q, s) >= 0, 1.0, 0.0)
            wet[s, :, at(q)] = jnp.broadcast_to(
                jnp.where(land[s, :, at(q)] > 0, held, 0.0), (layers, LANES)
            )
            head = h[s, :, at(q)]
            hh[s, :, at(q)] = head + (elev[s, :, at(q)] - depth)
            conductivity(s, q, head)
        return carry

    def balance(parts, s, carry):
        found = picks(s, parts)
        for q in parts:
            side = found[section(q)]
            k0, k_w, k_e, k_n, k_s = around(kk, s, q, found)
            h0, h_w, h_e, h_n, h_s = around(hh, s, q, found)
            mask_w = jnp.where(at_west, side[0][1], 1.0)
            mask_e = jnp.where(at_east, side[1][1], 1.0)
            mask_n = mask_s = None
            if q in (hc, nq - hc):
                mask_n = jnp.where(at_north, side[2][1], 1.0)
            if q == 0:
                mask_n = jnp.where(at_north, 0.0, 1.0)
            if q in (hc - 1, nq - hc - 1):
                mask_s = jnp.where(at_south, side[3][1], 1.0)
            if q == nq - 1:
                mask_s = jnp.where(at_south, 0.0, 1.0)
            inflow = None
            for k_j, h_j, mask, k_ref, g_ref in (
                (k_w, h_w, mask_w, kf_w, g_w),
                (k_e, h_e, mask_e, kf_e, g_e),
                (k_n, h_n, mask_n, kf_n, g_n),
                (k_s, h_s, mask_s, kf_s, g_s),
            ):
                face, drop = k0 + k_j, h_j - h0
                weighted = drop
                if mask is not None:
                    face, weighted = face * mask, drop * mask
                k_ref[s, :, at(q)] = face
                g_ref[s, :, at(q)] = weighted
                flow = face * drop
                inflow = flow if inflow is None else inflow + flow
                total = face if k_ref is kf_w else total + face
            drop = pltpu.roll(h0, 1, 0) - h0
            face = (k0 + pltpu.roll(k0, 1, 0)) * upper
            kf_u[s, :, at(q)] = face
            g_u[s, :, at(q)] = drop * upper
            flow = face * drop
            inflow = inflow + flow - pltpu.roll(flow, layers - 1, 0)
            total = total + face + pltpu.roll(face, layers - 1, 0)
            head = h[s, :, at(q)]
            shape = alpha[s, :, at(q)]
            pore = poro[s, :, at(q)]
            bend = jnp.tanh(shape * head)
            storage = 0.25 + pore * shape * (1.0 - bend * bend)
            residual = 0.25 * head + pore * bend - cst[s, :, at(q)] - inflow
            scaled = wet[s, :, at(q)] * inverse(storage + total)
            move = scaled * residual
            wi[s, :, at(q)] = scaled
            step[s, :, at(q)] = move
            qq[s, :, at(q)] = kp[s, :, at(q)] * move
        return carry

    def advance(parts, final, s, carry):
        found = picks(s, parts)
        for q in parts:
            s0, s_w, s_e, s_n, s_s = around(step, s, q, found)
            q0, q_w, q_e, q_n, q_s = around(qq, s, q, found)
            gsum = acc = None
            for s_j, q_j, k_ref, g_ref in (
                (s_w, q_w, kf_w, g_w),
                (s_e, q_e, kf_e, g_e),
                (s_n, q_n, kf_n, g_n),
                (s_s, q_s, kf_s, g_s),
            ):
                grad = g_ref[s, :, at(q)]
                term = k_ref[s, :, at(q)] * s_j + grad * q_j
                acc = term if acc is None else acc + term
                gsum = grad if gsum is None else gsum + grad
            face, grad = kf_u[s, :, at(q)], g_u[s, :, at(q)]
            acc = acc + face * pltpu.roll(s0, 1, 0) + grad * pltpu.roll(q0, 1, 0)
            acc = acc + pltpu.roll(face * s0 - grad * q0, layers - 1, 0)
            gsum = gsum + grad - pltpu.roll(grad, layers - 1, 0)
            change = s0 + wi[s, :, at(q)] * (acc + q0 * gsum)
            head = h[s, :, at(q)] - change
            h[s, :, at(q)] = head
            if final:
                strength = 2.0 * wet[s, :, at(q)] * (sat[s, :, at(q)] * (1.0 + jnp.tanh(head)))
                half, part = divmod(q - hc, HALO // LANES)
                flux[s * 4 + half, :, pl.ds(part * LANES, LANES)] = strength[0:1]
            else:
                hh[s, :, at(q)] = hh[s, :, at(q)] - change
                conductivity(s, q, head)
        return carry

    lax.fori_loop(0, slots, functools.partial(prepare, range(hc, nq - hc)), 0)
    inner = tuple(range(hc + 1, nq - hc - 1))
    lax.fori_loop(0, slots, functools.partial(balance, inner), 0)

    quarter = flux.shape[-1]
    place = lax.broadcasted_iota(jnp.int32, (n, LANES), 0) * atm

    def name(s, label):
        for k in range(4):
            there = own_atm[0, k, s] - place
            hit = (there >= 0) & (there < atm)
            label = jnp.where(hit, (there + 1).astype(jnp.float32), label)
        return label

    label = lax.fori_loop(0, slots, name, jnp.zeros((n, LANES), jnp.float32))
    for d in range(n):
        snd[d, :, pl.ds(quarter, LANES)] = label[d : d + 1]

    @pl.when(me > 0)
    def _():
        for copy in halo_copies(0):
            copy.wait_recv()

    @pl.when(me < n - 1)
    def _():
        for copy in halo_copies(1):
            copy.wait_recv()

    tabs = [
        pltpu.make_async_copy(src, dst, tab_sem.at[i])
        for i, (src, dst) in enumerate(
            (
                (north_nb_vec, north_nb),
                (south_nb_vec, south_nb),
                (north_tile_vec, north_tile),
                (south_tile_vec, south_tile),
            )
        )
    ]
    for copy in tabs:
        copy.start()
    for copy in tabs:
        copy.wait()

    halo_parts = tuple(range(hc)) + tuple(range(nq - hc, nq))
    lax.fori_loop(0, slots, functools.partial(prepare, halo_parts), 0)


    rows_per = LANES // TS
    for number in range(ITERS):
        rows_a = 2 * ITERS - 1 - 2 * number
        rows_b = rows_a - 1
        wide_a, wide_b = -(-rows_a // rows_per), -(-rows_b // rows_per)
        parts_a = range(hc - wide_a, nq - hc + wide_a)
        if number == 0:
            parts_a = tuple(q for q in parts_a if q not in inner)
        parts_b = range(hc - wide_b, nq - hc + wide_b)
        lax.fori_loop(0, slots, functools.partial(balance, parts_a), 0)
        lax.fori_loop(
            0, slots, functools.partial(advance, parts_b, number == ITERS - 1), 0
        )

    head_out = pltpu.make_async_copy(h.at[:, :, own], p_out.at[0], out_sem.at[0])
    head_out.start()

    wide_place = lax.broadcasted_iota(jnp.int32, (n, quarter), 0) * atm

    def collect(s, sums):
        for k in range(4):
            there = own_atm[0, k, s] - wide_place
            hit = (there >= 0) & (there < atm)
            sums = sums + jnp.where(hit, flux[s * 4 + k], 0.0)
        return sums

    sums = lax.fori_loop(0, slots, collect, jnp.zeros((n, quarter), jnp.float32))
    for d in range(n):
        snd[d, :, pl.ds(0, quarter)] = sums[d : d + 1]

    def exchange(src, dst, s_sem, r_sem):
        def one(o):
            peer = lax.rem(me + o, n)
            return pltpu.make_async_remote_copy(
                src_ref=src.at[peer],
                dst_ref=dst.at[me],
                send_sem=s_sem,
                recv_sem=r_sem,
                device_id=(group, peer),
                device_id_type=MESH,
            )

        def begin(o, carry):
            one(o).start()
            return carry

        lax.fori_loop(1, n, begin, 0, unroll=n <= 32)
        dst[me] = src[me]
        everyone = pltpu.make_async_copy(
            src.at[pl.ds(0, n - 1)], dst.at[pl.ds(0, n - 1)], r_sem
        )
        everyone.wait()
        return lambda: pltpu.make_async_copy(
            src.at[pl.ds(0, n - 1)], dst.at[pl.ds(0, n - 1)], s_sem
        ).wait()

    finish_a = exchange(snd, rcv, a_send, a_recv)

    for d in range(n):
        rows[d : d + 1, :] = rcv[d]
    got = rows[:, pl.ds(0, quarter)]
    tag = rows[:, pl.ds(quarter, LANES)]
    tag = jnp.concatenate([tag] * (quarter // LANES), axis=1)

    back = jnp.zeros((n, quarter), jnp.float32)
    for a in range(atm):
        hit = tag == float(a + 1)
        total = jnp.sum(jnp.where(hit, got, 0.0), axis=0, keepdims=True)
        count = jnp.sum(jnp.where(hit, 2.0, 0.0), axis=0, keepdims=True)
        mean = total / jnp.maximum(count, 1.0)
        demand = forcing[0, a : a + 1, :]
        supply = forcing[1, a : a + 1, :]
        rate = supply - demand * mean / (mean + demand)
        back = jnp.where(hit, rate, back)

    for d in range(n):
        snd2[d] = back[d : d + 1]
    finish_b = exchange(snd2, rcv2, b_send, b_recv)

    def settle(s, carry):
        for k in range(4):
            number = own_atm[0, k, s]
            live = jnp.where(number >= 0, 1.0, 0.0)
            rate = rcv2[lax.div(jnp.maximum(number, 0), atm)] * live
            ret[0, s, pl.ds(k, 1), :] = rate
            for part in range(quarter // LANES):
                q = k * (quarter // LANES) + part
                piece = rate[:, part * LANES : (part + 1) * LANES]
                added[s, :, at(q)] = COUPLING * wet[s, 0:1, at(hc + q)] * piece
        return carry

    lax.fori_loop(0, slots, settle, 0)
    outs = [
        pltpu.make_async_copy(added, added_out, out_sem.at[1]),
        pltpu.make_async_copy(ret, ret_out, out_sem.at[2]),
    ]
    for copy in outs:
        copy.start()
    finish_a()
    finish_b()

    @pl.when(me < n - 1)
    def _():
        for copy in halo_copies(0):
            copy.wait_send()

    @pl.when(me > 0)
    def _():
        for copy in halo_copies(1):
            copy.wait_send()

    head_out.wait()
    for copy in outs:
        copy.wait()


def couple_kernel(
    head_in, added_in, rate_in, head_out, rate_out, head, added, rate, in_sem, out_sem, side_sem
):
    slots = head.shape[0]
    loads = [
        pltpu.make_async_copy(head_in.at[0, s], head.at[s], in_sem.at[s]) for s in range(slots)
    ]
    stores = [
        pltpu.make_async_copy(head.at[s], head_out.at[0, s], out_sem.at[s]) for s in range(slots)
    ]
    load_added = pltpu.make_async_copy(added_in, added, side_sem.at[0])
    load_rate = pltpu.make_async_copy(rate_in, rate, side_sem.at[1])
    store_rate = pltpu.make_async_copy(rate, rate_out, side_sem.at[2])
    load_added.start()
    for copy in loads:
        copy.start()
    load_rate.start()
    load_added.wait()
    for s in range(slots):
        loads[s].wait()
        head[s, 0:1, :] = head[s, 0:1, :] + added[s]
        stores[s].start()
    load_rate.wait()
    store_rate.start()
    for copy in stores:
        copy.wait()
    store_rate.wait()


def couple(head, added, rate):
    dma = pltpu.SemaphoreType.DMA
    slots = head.shape[1]
    anywhere = pl.BlockSpec(memory_space=pl.ANY)
    return pl.pallas_call(
        couple_kernel,
        out_shape=[jax.ShapeDtypeStruct(v.shape, v.dtype) for v in (head, rate)],
        in_specs=[anywhere] * 3,
        out_specs=[anywhere] * 2,
        scratch_shapes=[
            pltpu.VMEM(head.shape[1:], head.dtype),
            pltpu.VMEM(added.shape, added.dtype),
            pltpu.VMEM(rate.shape, rate.dtype),
            dma((slots,)),
            dma((slots,)),
            dma((3,)),
        ],
        compiler_params=pltpu.CompilerParams(vmem_limit_bytes=60 * 2**20),
    )(head, added, rate)


def on_device(n, *args):
    (pressure, pressure_old, soil, elev, land, rain, tiles, neighbors, atm_map, forcing) = args
    _, slots, layers, cells = pressure.shape
    quarter = cells // 4
    wide = cells + 2 * HALO
    elev, land, rain = (jnp.transpose(v, (1, 0, 2)) for v in (elev, land, rain))
    neighbors, atm_map = (jnp.transpose(v, (0, 2, 1)) for v in (neighbors, atm_map))
    vec, smem, anywhere = pltpu.VMEM, pltpu.SMEM, pl.ANY

    def cube(kind=jnp.float32):
        return vec((slots, layers, wide), kind)

    def lines(kind=jnp.float32):
        return vec((slots, 1, wide), kind)

    dma = pltpu.SemaphoreType.DMA
    made = pl.pallas_call(
        functools.partial(kernel, n),
        out_shape=[
            jax.ShapeDtypeStruct(pressure.shape, jnp.float32),
            jax.ShapeDtypeStruct((slots, 1, cells), jnp.float32),
            jax.ShapeDtypeStruct((1, slots, 4, quarter), jnp.float32),
        ],
        in_specs=[pl.BlockSpec(memory_space=anywhere)] * 10,
        out_specs=[pl.BlockSpec(memory_space=anywhere)] * 3,
        scratch_shapes=[
            cube(),
            cube(),
            cube(jnp.int32),
            lines(),
            lines(jnp.int32),
            lines(),
            vec((1, 4, slots), jnp.int32),
            vec((1, 4, slots), jnp.int32),
            vec((1, slots), jnp.int32),
            vec((1, slots), jnp.int32),
            smem((1, 4, slots), jnp.int32),
            smem((1, 4, slots), jnp.int32),
            smem((1, slots), jnp.int32),
            smem((1, slots), jnp.int32),
            smem((1, 4, slots), jnp.int32),
            smem((1, slots), jnp.int32),
            smem((1, 4, slots), jnp.int32),
            vec(forcing.shape, jnp.float32),
            vec((1, slots, 4, quarter), jnp.float32),
            vec((slots, 1, cells), jnp.float32),
        ]
        + [cube()] * 20
        + [
            vec((slots * 4, 1, quarter), jnp.float32),
            vec((n, quarter + LANES), jnp.float32),
            vec((n, 1, quarter + LANES), jnp.float32),
            vec((n, 1, quarter + LANES), jnp.float32),
            vec((n, 1, quarter), jnp.float32),
            vec((n, 1, quarter), jnp.float32),
            dma((10,)),
            dma((2, 8)),
            dma((2, 8)),
            dma((4,)),
            dma,
            dma,
            dma,
            dma,
            dma((3,)),
        ],
        compiler_params=pltpu.CompilerParams(
            collective_id=0, has_side_effects=True, vmem_limit_bytes=60 * 2**20
        ),
    )(pressure, pressure_old, soil, elev, land, rain, neighbors, tiles, atm_map, forcing)
    return tuple(couple(*made))


def solution(mesh):
    both = ("group", "tx")
    in_specs = (
        P(both, None, None, None),
        P(both, None, None, None),
        P("tx", None, None, None),
        P("tx", None, None),
        P("tx", None, None),
        P(both, None, None),
        P("tx", None),
        P("tx", None, None),
        P("tx", None, None),
        P(None, both, None),
    )
    out_specs = [P(both, None, None, None), P(both, None, None, None)]
    return jax.shard_map(
        functools.partial(on_device, mesh.shape["tx"]),
        mesh=mesh,
        in_specs=in_specs,
        out_specs=tuple(out_specs),
        check_vma=False,
    )
```

```python
import functools

import jax
import jax.numpy as jnp
import numpy as np
from jax import lax
from jax.experimental import pallas as pl
from jax.experimental.pallas import tpu as pltpu
from jax.sharding import PartitionSpec as P

TS = 32
LAG_PREPARE, LAG_BALANCE, LAG_ADVANCE = 3, 2, 3
ITERS = 4
LANES = 128
HALO = 2 * ITERS * TS

KSAT = np.array(
    [0.4, 0.32, 0.26, 0.21, 0.17, 0.14, 0.115, 0.095, 0.08, 0.067, 0.057, 0.05], np.float32
)
SHAPE = np.array([3.0, 2.6, 2.2, 1.9, 1.6, 1.4, 1.2, 1.0, 0.9, 0.8, 0.7, 0.6], np.float32)
POROSITY = np.array(
    [0.38, 0.39, 0.4, 0.43, 0.45, 0.41, 0.39, 0.43, 0.44, 0.38, 0.46, 0.48], np.float32
)
LAYER_DROP = 0.25
COUPLING = 0.5
MESH = pl.DeviceIdType.MESH


class Later:
    def __init__(self, lag):
        self.lag, self.held, self.now = lag, [], []

    def put(self, ref, place, value):
        self.now.append((ref, place, value))

    def close(self):
        self.held.append(self.now)
        self.now = []
        if len(self.held) > self.lag:
            self.write(self.held.pop(0))

    def write(self, stores):
        for ref, place, value in stores:
            ref[place] = value

    def flush(self):
        for stores in self.held:
            self.write(stores)


def inverse(v):
    guess = pl.reciprocal(v, approx=True)
    return guess * (2.0 - v * guess)


def kernel(
    n,
    p_in,
    old_in,
    soil_in,
    elev_in,
    land_in,
    rain_in,
    nb_in,
    tile_in,
    atm_in,
    forcing_in,
    p_out,
    added_out,
    ret_out,
    h,
    cst,
    soil,
    elev,
    land,
    rain,
    north_nb_vec,
    south_nb_vec,
    north_tile_vec,
    south_tile_vec,
    north_nb,
    south_nb,
    north_tile,
    south_tile,
    own_nb,
    own_tile,
    own_atm,
    forcing,
    ret,
    added,
    kk,
    kp,
    hh,
    step,
    qq,
    wi,
    sat,
    alpha,
    poro,
    wet,
    kf_w,
    kf_e,
    kf_n,
    kf_s,
    kf_u,
    g_w,
    g_e,
    g_n,
    g_s,
    g_u,
    flux,
    rows,
    snd,
    rcv,
    snd2,
    rcv2,
    local_sem,
    send_sem,
    recv_sem,
    tab_sem,
    a_send,
    a_recv,
    b_send,
    b_recv,
    out_sem,
):
    me = lax.axis_index("tx")
    group = lax.axis_index("group")
    slots, layers = h.shape[0], h.shape[1]
    cells = p_in.shape[-1]
    own = pl.ds(HALO, cells)
    top_part, low_part = pl.ds(0, HALO), pl.ds(HALO + cells, HALO)
    atm = forcing.shape[1]
    hc = HALO // LANES
    nq = (cells + 2 * HALO) // LANES

    big = [(p_in, h), (old_in, cst), (soil_in, soil)]
    small = [(elev_in, elev), (land_in, land), (rain_in, rain)]
    local = []
    for src, dst in big:
        local.append((src.at[0], dst.at[:, :, own]))
    for src, dst in small:
        local.append((src, dst.at[:, :, own]))
    local += [(nb_in, own_nb), (tile_in, own_tile), (atm_in, own_atm), (forcing_in, forcing)]
    locals_ = [
        pltpu.make_async_copy(src, dst, local_sem.at[i]) for i, (src, dst) in enumerate(local)
    ]
    for copy in locals_:
        copy.start()

    for part in (top_part, low_part):
        for _, dst in big:
            dst[:, :, part] = jnp.zeros((slots, layers, HALO), dst.dtype)
        for _, dst in small:
            dst[:, :, part] = jnp.zeros((slots, 1, HALO), dst.dtype)
    for dst in (north_nb_vec, south_nb_vec, north_tile_vec, south_tile_vec):
        dst[...] = jnp.zeros(dst.shape, jnp.int32)

    barrier = pltpu.get_barrier_semaphore()

    def greet(o, carry):
        pl.semaphore_signal(
            barrier, inc=1, device_id=(group, lax.rem(me + o, n)), device_id_type=MESH
        )
        return carry

    lax.fori_loop(1, n, greet, 0, unroll=n <= 32)
    pl.semaphore_wait(barrier, n - 1)

    def halo_copies(way):
        src_part = pl.ds(cells - HALO, HALO) if way == 0 else pl.ds(0, HALO)
        dst_part = top_part if way == 0 else low_part
        pairs = [
            (nb_in, north_nb_vec if way == 0 else south_nb_vec),
            (tile_in, north_tile_vec if way == 0 else south_tile_vec),
        ]
        pairs += [(src.at[:, :, src_part], dst.at[:, :, dst_part]) for src, dst in small]
        pairs += [(src.at[0, :, :, src_part], dst.at[:, :, dst_part]) for src, dst in big]
        target = me + 1 if way == 0 else me - 1
        return [
            pltpu.make_async_remote_copy(
                src_ref=src,
                dst_ref=dst,
                send_sem=send_sem.at[way, i],
                recv_sem=recv_sem.at[way, i],
                device_id=(group, target),
                device_id_type=MESH,
            )
            for i, (src, dst) in enumerate(pairs)
        ]

    @pl.when(me < n - 1)
    def _():
        for copy in halo_copies(0):
            copy.start()

    @pl.when(me > 0)
    def _():
        for copy in halo_copies(1):
            copy.start()

    for copy in locals_:
        copy.wait()

    lane = lax.broadcasted_iota(jnp.int32, (layers, LANES), 1)
    layer = lax.broadcasted_iota(jnp.int32, (layers, LANES), 0)
    x_place = lax.rem(lane, TS)
    at_west, at_east = x_place == 0, x_place == TS - 1
    at_north, at_south = lane < TS, lane >= LANES - TS
    depth = layer.astype(jnp.float32) * LAYER_DROP
    upper = jnp.where(layer > 0, 2.0, 0.0)

    def at(q):
        return pl.ds(q * LANES, LANES)

    def neighbor(q, s, f):
        if hc <= q < nq - hc:
            return own_nb[0, f, s]
        return (north_nb if q < hc else south_nb)[0, f, s]

    def tile(q, s):
        return (north_tile if q < hc else (own_tile if q < nq - hc else south_tile))[0, s]

    def picks(s, parts):
        found = {}
        for sec, q in ((0, 0), (1, hc), (2, nq - hc)):
            if all(section(part) != sec for part in parts):
                continue
            side = []
            for f in range(4):
                number = neighbor(q, s, f)
                side.append((jnp.maximum(number, 0), jnp.where(number >= 0, 1.0, 0.0)))
            found[sec] = side
        return found

    def section(q):
        return 0 if q < hc else (1 if q < nq - hc else 2)

    def around(field, s, q, found):
        side = found[section(q)]
        mid = field[s, :, at(q)]
        west = jnp.where(
            at_west,
            pltpu.roll(field[side[0][0], :, at(q)], LANES - TS + 1, 1),
            pltpu.roll(mid, 1, 1),
        )
        east = jnp.where(
            at_east,
            pltpu.roll(field[side[1][0], :, at(q)], TS - 1, 1),
            pltpu.roll(mid, LANES - 1, 1),
        )
        north_slot = side[2][0] if q in (hc, nq - hc) else s
        south_slot = side[3][0] if q in (hc - 1, nq - hc - 1) else s
        above = field[north_slot, :, at(max(q - 1, 0))]
        below = field[south_slot, :, at(min(q + 1, nq - 1))]
        north = pltpu.roll(jnp.where(at_south, above, mid), TS, 1)
        south = pltpu.roll(jnp.where(at_north, below, mid), LANES - TS, 1)
        return mid, west, east, north, south

    def conductivity(later, s, q, head, quarter_sat):
        bend = jnp.tanh(head)
        conduct = quarter_sat * (1.0 + bend)
        later.put(kk, (s, slice(None), at(q)), conduct)
        later.put(kp, (s, slice(None), at(q)), conduct * (1.0 - bend))

    def prepare(parts, s, carry):
        later = Later(LAG_PREPARE)
        for q in parts:
            classes = soil[s, :, at(q)]
            tables = [jnp.full((layers, LANES), float(t[0]), jnp.float32) for t in (KSAT, SHAPE, POROSITY)]
            for number in range(1, KSAT.shape[0]):
                hit = classes == number
                tables = [
                    jnp.where(hit, float(t[number]), v)
                    for t, v in zip((KSAT, SHAPE, POROSITY), tables)
                ]
            quarter_sat = 0.25 * tables[0]
            later.put(sat, (s, slice(None), at(q)), quarter_sat)
            half_shape, eighth = 0.5 * tables[1], 0.125 * tables[2]
            later.put(alpha, (s, slice(None), at(q)), half_shape)
            later.put(poro, (s, slice(None), at(q)), eighth)
            old = cst[s, :, at(q)]
            rain_top = jnp.where(layer == 0, rain[s, :, at(q)], 0.0)
            later.put(cst, (s, slice(None), at(q)), 0.25 * old + eighth * jnp.tanh(half_shape * old) + rain_top)
            held = jnp.where(tile(q, s) >= 0, 1.0, 0.0)
            damp = jnp.where(land[s, :, at(q)] > 0, held, 0.0)
            later.put(wet, (s, slice(None), at(q)), jnp.broadcast_to(damp, (layers, LANES)))
            head = h[s, :, at(q)]
            later.put(hh, (s, slice(None), at(q)), head + (elev[s, :, at(q)] - depth))
            conductivity(later, s, q, head, quarter_sat)
            later.close()
        later.flush()
        return carry

    def balance(parts, s, carry):
        later = Later(LAG_BALANCE)
        found = picks(s, parts)
        for q in parts:
            side = found[section(q)]
            k0, k_w, k_e, k_n, k_s = around(kk, s, q, found)
            h0, h_w, h_e, h_n, h_s = around(hh, s, q, found)
            mask_w = jnp.where(at_west, side[0][1], 1.0)
            mask_e = jnp.where(at_east, side[1][1], 1.0)
            mask_n = mask_s = None
            if q in (hc, nq - hc):
                mask_n = jnp.where(at_north, side[2][1], 1.0)
            if q == 0:
                mask_n = jnp.where(at_north, 0.0, 1.0)
            if q in (hc - 1, nq - hc - 1):
                mask_s = jnp.where(at_south, side[3][1], 1.0)
            if q == nq - 1:
                mask_s = jnp.where(at_south, 0.0, 1.0)
            inflow = None
            for k_j, h_j, mask, k_ref, g_ref in (
                (k_w, h_w, mask_w, kf_w, g_w),
                (k_e, h_e, mask_e, kf_e, g_e),
                (k_n, h_n, mask_n, kf_n, g_n),
                (k_s, h_s, mask_s, kf_s, g_s),
            ):
                face, drop = k0 + k_j, h_j - h0
                weighted = drop
                if mask is not None:
                    face, weighted = face * mask, drop * mask
                later.put(k_ref, (s, slice(None), at(q)), face)
                later.put(g_ref, (s, slice(None), at(q)), weighted)
                flow = face * drop
                inflow = flow if inflow is None else inflow + flow
                total = face if k_ref is kf_w else total + face
            drop = pltpu.roll(h0, 1, 0) - h0
            face = (k0 + pltpu.roll(k0, 1, 0)) * upper
            later.put(kf_u, (s, slice(None), at(q)), face)
            later.put(g_u, (s, slice(None), at(q)), drop * upper)
            flow = face * drop
            inflow = inflow + flow - pltpu.roll(flow, layers - 1, 0)
            total = total + face + pltpu.roll(face, layers - 1, 0)
            head = h[s, :, at(q)]
            shape = alpha[s, :, at(q)]
            pore = poro[s, :, at(q)]
            bend = jnp.tanh(shape * head)
            storage = 0.25 + pore * shape * (1.0 - bend * bend)
            residual = 0.25 * head + pore * bend - cst[s, :, at(q)] - inflow
            scaled = wet[s, :, at(q)] * inverse(storage + total)
            move = scaled * residual
            later.put(wi, (s, slice(None), at(q)), scaled)
            later.put(step, (s, slice(None), at(q)), move)
            later.put(qq, (s, slice(None), at(q)), kp[s, :, at(q)] * move)
            later.close()
        later.flush()
        return carry

    def advance(parts, final, s, carry):
        later = Later(LAG_ADVANCE)
        found = picks(s, parts)
        for q in parts:
            s0, s_w, s_e, s_n, s_s = around(step, s, q, found)
            q0, q_w, q_e, q_n, q_s = around(qq, s, q, found)
            gsum = acc = None
            for s_j, q_j, k_ref, g_ref in (
                (s_w, q_w, kf_w, g_w),
                (s_e, q_e, kf_e, g_e),
                (s_n, q_n, kf_n, g_n),
                (s_s, q_s, kf_s, g_s),
            ):
                grad = g_ref[s, :, at(q)]
                term = k_ref[s, :, at(q)] * s_j + grad * q_j
                acc = term if acc is None else acc + term
                gsum = grad if gsum is None else gsum + grad
            face, grad = kf_u[s, :, at(q)], g_u[s, :, at(q)]
            acc = acc + face * pltpu.roll(s0, 1, 0) + grad * pltpu.roll(q0, 1, 0)
            acc = acc + pltpu.roll(face * s0 - grad * q0, layers - 1, 0)
            gsum = gsum + grad - pltpu.roll(grad, layers - 1, 0)
            change = s0 + wi[s, :, at(q)] * (acc + q0 * gsum)
            head = h[s, :, at(q)] - change
            later.put(h, (s, slice(None), at(q)), head)
            if final:
                strength = 2.0 * wet[s, :, at(q)] * (sat[s, :, at(q)] * (1.0 + jnp.tanh(head)))
                half, part = divmod(q - hc, HALO // LANES)
                later.put(
                    flux, (s * 4 + half, slice(None), pl.ds(part * LANES, LANES)), strength[0:1]
                )
            else:
                later.put(hh, (s, slice(None), at(q)), hh[s, :, at(q)] - change)
                conductivity(later, s, q, head, sat[s, :, at(q)])
            later.close()
        later.flush()
        return carry

    lax.fori_loop(0, slots, functools.partial(prepare, range(hc, nq - hc)), 0)
    inner = tuple(range(hc + 1, nq - hc - 1))
    lax.fori_loop(0, slots, functools.partial(balance, inner), 0)

    quarter = flux.shape[-1]
    place = lax.broadcasted_iota(jnp.int32, (n, LANES), 0) * atm

    def name(s, label):
        for k in range(4):
            there = own_atm[0, k, s] - place
            hit = (there >= 0) & (there < atm)
            label = jnp.where(hit, (there + 1).astype(jnp.float32), label)
        return label

    label = lax.fori_loop(0, slots, name, jnp.zeros((n, LANES), jnp.float32))
    for d in range(n):
        snd[d, :, pl.ds(quarter, LANES)] = label[d : d + 1]

    @pl.when(me > 0)
    def _():
        for copy in halo_copies(0):
            copy.wait_recv()

    @pl.when(me < n - 1)
    def _():
        for copy in halo_copies(1):
            copy.wait_recv()

    tabs = [
        pltpu.make_async_copy(src, dst, tab_sem.at[i])
        for i, (src, dst) in enumerate(
            (
                (north_nb_vec, north_nb),
                (south_nb_vec, south_nb),
                (north_tile_vec, north_tile),
                (south_tile_vec, south_tile),
            )
        )
    ]
    for copy in tabs:
        copy.start()
    for copy in tabs:
        copy.wait()

    halo_parts = tuple(range(hc)) + tuple(range(nq - hc, nq))
    lax.fori_loop(0, slots, functools.partial(prepare, halo_parts), 0)


    rows_per = LANES // TS
    for number in range(ITERS):
        rows_a = 2 * ITERS - 1 - 2 * number
        rows_b = rows_a - 1
        wide_a, wide_b = -(-rows_a // rows_per), -(-rows_b // rows_per)
        parts_a = range(hc - wide_a, nq - hc + wide_a)
        if number == 0:
            parts_a = tuple(q for q in parts_a if q not in inner)
        parts_b = range(hc - wide_b, nq - hc + wide_b)
        lax.fori_loop(0, slots, functools.partial(balance, parts_a), 0)
        lax.fori_loop(
            0, slots, functools.partial(advance, parts_b, number == ITERS - 1), 0
        )

    head_out = pltpu.make_async_copy(h.at[:, :, own], p_out.at[0], out_sem.at[0])
    head_out.start()

    wide_place = lax.broadcasted_iota(jnp.int32, (n, quarter), 0) * atm

    def collect(s, sums):
        for k in range(4):
            there = own_atm[0, k, s] - wide_place
            hit = (there >= 0) & (there < atm)
            sums = sums + jnp.where(hit, flux[s * 4 + k], 0.0)
        return sums

    sums = lax.fori_loop(0, slots, collect, jnp.zeros((n, quarter), jnp.float32))
    for d in range(n):
        snd[d, :, pl.ds(0, quarter)] = sums[d : d + 1]

    def exchange(src, dst, s_sem, r_sem):
        def one(o):
            peer = lax.rem(me + o, n)
            return pltpu.make_async_remote_copy(
                src_ref=src.at[peer],
                dst_ref=dst.at[me],
                send_sem=s_sem,
                recv_sem=r_sem,
                device_id=(group, peer),
                device_id_type=MESH,
            )

        def begin(o, carry):
            one(o).start()
            return carry

        lax.fori_loop(1, n, begin, 0, unroll=n <= 32)
        dst[me] = src[me]
        everyone = pltpu.make_async_copy(
            src.at[pl.ds(0, n - 1)], dst.at[pl.ds(0, n - 1)], r_sem
        )
        everyone.wait()
        return lambda: pltpu.make_async_copy(
            src.at[pl.ds(0, n - 1)], dst.at[pl.ds(0, n - 1)], s_sem
        ).wait()

    finish_a = exchange(snd, rcv, a_send, a_recv)

    for d in range(n):
        rows[d : d + 1, :] = rcv[d]
    got = rows[:, pl.ds(0, quarter)]
    tag = rows[:, pl.ds(quarter, LANES)]
    tag = jnp.concatenate([tag] * (quarter // LANES), axis=1)

    back = jnp.zeros((n, quarter), jnp.float32)
    for a in range(atm):
        hit = tag == float(a + 1)
        total = jnp.sum(jnp.where(hit, got, 0.0), axis=0, keepdims=True)
        count = jnp.sum(jnp.where(hit, 2.0, 0.0), axis=0, keepdims=True)
        mean = total / jnp.maximum(count, 1.0)
        demand = forcing[0, a : a + 1, :]
        supply = forcing[1, a : a + 1, :]
        rate = supply - demand * mean / (mean + demand)
        back = jnp.where(hit, rate, back)

    for d in range(n):
        snd2[d] = back[d : d + 1]
    finish_b = exchange(snd2, rcv2, b_send, b_recv)

    def settle(s, carry):
        for k in range(4):
            number = own_atm[0, k, s]
            live = jnp.where(number >= 0, 1.0, 0.0)
            rate = rcv2[lax.div(jnp.maximum(number, 0), atm)] * live
            ret[0, s, pl.ds(k, 1), :] = rate
            for part in range(quarter // LANES):
                q = k * (quarter // LANES) + part
                piece = rate[:, part * LANES : (part + 1) * LANES]
                added[s, :, at(q)] = COUPLING * wet[s, 0:1, at(hc + q)] * piece
        return carry

    lax.fori_loop(0, slots, settle, 0)
    outs = [
        pltpu.make_async_copy(added, added_out, out_sem.at[1]),
        pltpu.make_async_copy(ret, ret_out, out_sem.at[2]),
    ]
    for copy in outs:
        copy.start()
    finish_a()
    finish_b()

    @pl.when(me < n - 1)
    def _():
        for copy in halo_copies(0):
            copy.wait_send()

    @pl.when(me > 0)
    def _():
        for copy in halo_copies(1):
            copy.wait_send()

    head_out.wait()
    for copy in outs:
        copy.wait()


def couple_kernel(
    head_in, added_in, rate_in, head_out, rate_out, head, added, rate, in_sem, out_sem, side_sem
):
    slots = head.shape[0]
    loads = [
        pltpu.make_async_copy(head_in.at[0, s], head.at[s], in_sem.at[s]) for s in range(slots)
    ]
    stores = [
        pltpu.make_async_copy(head.at[s], head_out.at[0, s], out_sem.at[s]) for s in range(slots)
    ]
    load_added = pltpu.make_async_copy(added_in, added, side_sem.at[0])
    load_rate = pltpu.make_async_copy(rate_in, rate, side_sem.at[1])
    store_rate = pltpu.make_async_copy(rate, rate_out, side_sem.at[2])
    load_added.start()
    for copy in loads:
        copy.start()
    load_rate.start()
    load_added.wait()
    for s in range(slots):
        loads[s].wait()
        head[s, 0:1, :] = head[s, 0:1, :] + added[s]
        stores[s].start()
    load_rate.wait()
    store_rate.start()
    for copy in stores:
        copy.wait()
    store_rate.wait()


def couple(head, added, rate):
    dma = pltpu.SemaphoreType.DMA
    slots = head.shape[1]
    anywhere = pl.BlockSpec(memory_space=pl.ANY)
    return pl.pallas_call(
        couple_kernel,
        out_shape=[jax.ShapeDtypeStruct(v.shape, v.dtype) for v in (head, rate)],
        in_specs=[anywhere] * 3,
        out_specs=[anywhere] * 2,
        scratch_shapes=[
            pltpu.VMEM(head.shape[1:], head.dtype),
            pltpu.VMEM(added.shape, added.dtype),
            pltpu.VMEM(rate.shape, rate.dtype),
            dma((slots,)),
            dma((slots,)),
            dma((3,)),
        ],
        compiler_params=pltpu.CompilerParams(vmem_limit_bytes=60 * 2**20),
    )(head, added, rate)


def on_device(n, *args):
    (pressure, pressure_old, soil, elev, land, rain, tiles, neighbors, atm_map, forcing) = args
    _, slots, layers, cells = pressure.shape
    quarter = cells // 4
    wide = cells + 2 * HALO
    elev, land, rain = (jnp.transpose(v, (1, 0, 2)) for v in (elev, land, rain))
    neighbors, atm_map = (jnp.transpose(v, (0, 2, 1)) for v in (neighbors, atm_map))
    vec, smem, anywhere = pltpu.VMEM, pltpu.SMEM, pl.ANY

    def cube(kind=jnp.float32):
        return vec((slots, layers, wide), kind)

    def lines(kind=jnp.float32):
        return vec((slots, 1, wide), kind)

    dma = pltpu.SemaphoreType.DMA
    made = pl.pallas_call(
        functools.partial(kernel, n),
        out_shape=[
            jax.ShapeDtypeStruct(pressure.shape, jnp.float32),
            jax.ShapeDtypeStruct((slots, 1, cells), jnp.float32),
            jax.ShapeDtypeStruct((1, slots, 4, quarter), jnp.float32),
        ],
        in_specs=[pl.BlockSpec(memory_space=anywhere)] * 10,
        out_specs=[pl.BlockSpec(memory_space=anywhere)] * 3,
        scratch_shapes=[
            cube(),
            cube(),
            cube(jnp.int32),
            lines(),
            lines(jnp.int32),
            lines(),
            vec((1, 4, slots), jnp.int32),
            vec((1, 4, slots), jnp.int32),
            vec((1, slots), jnp.int32),
            vec((1, slots), jnp.int32),
            smem((1, 4, slots), jnp.int32),
            smem((1, 4, slots), jnp.int32),
            smem((1, slots), jnp.int32),
            smem((1, slots), jnp.int32),
            smem((1, 4, slots), jnp.int32),
            smem((1, slots), jnp.int32),
            smem((1, 4, slots), jnp.int32),
            vec(forcing.shape, jnp.float32),
            vec((1, slots, 4, quarter), jnp.float32),
            vec((slots, 1, cells), jnp.float32),
        ]
        + [cube()] * 20
        + [
            vec((slots * 4, 1, quarter), jnp.float32),
            vec((n, quarter + LANES), jnp.float32),
            vec((n, 1, quarter + LANES), jnp.float32),
            vec((n, 1, quarter + LANES), jnp.float32),
            vec((n, 1, quarter), jnp.float32),
            vec((n, 1, quarter), jnp.float32),
            dma((10,)),
            dma((2, 8)),
            dma((2, 8)),
            dma((4,)),
            dma,
            dma,
            dma,
            dma,
            dma((3,)),
        ],
        compiler_params=pltpu.CompilerParams(
            collective_id=0, has_side_effects=True, vmem_limit_bytes=60 * 2**20
        ),
    )(pressure, pressure_old, soil, elev, land, rain, neighbors, tiles, atm_map, forcing)
    return tuple(couple(*made))


def solution(mesh):
    both = ("group", "tx")
    in_specs = (
        P(both, None, None, None),
        P(both, None, None, None),
        P("tx", None, None, None),
        P("tx", None, None),
        P("tx", None, None),
        P(both, None, None),
        P("tx", None),
        P("tx", None, None),
        P("tx", None, None),
        P(None, both, None),
    )
    out_specs = [P(both, None, None, None), P(both, None, None, None)]
    return jax.shard_map(
        functools.partial(on_device, mesh.shape["tx"]),
        mesh=mesh,
        in_specs=in_specs,
        out_specs=tuple(out_specs),
        check_vma=False,
    )
```
